128 devices in a mesh: lab: 16 (over z, x), fleet: 8 (over y, core).
Axes of the slice: x: 4, y: 4, z: 4, core: 2. Of those that a mesh axis runs over, the one named last changes fastest.
Arguments:
- lab_features: bfloat16 [64, 32768], P(None, ('lab', 'fleet')), may hold values from -4 to 4
- fleet_features: bfloat16 [64, 32768], P(None, ('fleet', 'lab')), may hold values from -4 to 4
- lab_weight: float32 [32768], P('lab'), may hold values from 0.5 to 2
- fleet_weight: float32 [32768], P('fleet'), may hold values from 0.5 to 2
Outputs:
- lab_potential: float32 [32768], P('lab')
- fleet_potential: float32 [32768], P('fleet')
- fleet_gradient: float32 [64, 32768], P(None, ('fleet', 'lab'))
The draws below stay inside these ranges and needn't reach their ends.
All inputs are finite; a program needn't handle non-finite values.
Results may differ from the reference program's by a relative error of at most 0.0003.
Values may be sent and summed in bfloat16 or wider, within the bound.
A program may use at most 128 MiB of HBM per device.

```python
import math
import jax
import jax.numpy as jnp
from jax import lax

FEATURES = 64
ITERS = 3
LAB_ROWS = 32768
FLEET_ROWS = 32768


def draw_lab_features(key, part):
    key = jax.random.fold_in(key, 11)
    first = jax.random.fold_in(key, 0)
    base = jnp.clip(jax.random.normal(first, (FEATURES, LAB_ROWS), jnp.float32), -6.0, 6.0)
    return (0.25 * base).astype(jnp.bfloat16)


def draw_fleet_features(key, part):
    key = jax.random.fold_in(key, 12)
    first = jax.random.fold_in(key, 0)
    base = jnp.clip(jax.random.normal(first, (FEATURES, FLEET_ROWS), jnp.float32), -6.0, 6.0)
    return (0.25 * base).astype(jnp.bfloat16)


def shard_levels(key, dims, cuts, smallest, high):
    gain = 1.0
    for axis_at, parts in cuts:
        draws = jax.random.uniform(jax.random.fold_in(jax.random.fold_in(key, 6), axis_at), (parts,), jnp.float32, smallest / len(cuts), high / len(cuts))
        gain = gain * jnp.repeat(jnp.exp(draws), dims[axis_at] // parts).reshape((-1,) + (1,) * (len(dims) - 1 - axis_at))
    return gain


def setup_inputs(seed: int = 0) -> dict:
    splits = jax.random.split(jax.random.key(seed), 5)
    return {
        "lab_features": draw_lab_features(jax.random.fold_in(splits[4], 71), 0),
        "fleet_features": draw_fleet_features(jax.random.fold_in(splits[4], 71), 0),
        "lab_weight": jnp.clip(jnp.exp(math.log(2.0) - 1.3862944 * jax.random.uniform(splits[2], (LAB_ROWS,), jnp.float32) ** shard_levels(splits[2], (LAB_ROWS,), ((0, 16),), -0.2, 0.2)), 0.5, 2.0),
        "fleet_weight": jnp.clip(jnp.exp(math.log(2.0) - 1.3862944 * jax.random.uniform(splits[3], (FLEET_ROWS,), jnp.float32) ** shard_levels(splits[3], (FLEET_ROWS,), ((0, 8),), -0.2, 0.2)), 0.5, 2.0),
    }


EPS = 0.5


def block_width(count):
    return 512 if count % 512 == 0 else count


def split_columns(array, width):
    return array.reshape(array.shape[0], array.shape[1] // width, width).transpose(1, 0, 2)


def pair_cost(lab_part, sq_lab_part, fleet_part, sq_fleet_part):
    cross = lax.dot_general(lab_part, fleet_part, (((0,), (0,)), ((), ())), preferred_element_type=jnp.float32)
    return sq_lab_part[:, None] + sq_fleet_part[None, :] - 2.0 * cross


def reference(lab_features, fleet_features, lab_weight, fleet_weight):
    lab_float = lab_features.astype(jnp.float32)
    fleet_float = fleet_features.astype(jnp.float32)
    sq_lab = jnp.sum(lab_float * lab_float, axis=0)
    sq_fleet = jnp.sum(fleet_float * fleet_float, axis=0)
    log_a = jnp.log(lab_weight)
    log_b = jnp.log(fleet_weight)
    lab_count = lab_features.shape[1]
    fleet_count = fleet_features.shape[1]
    lab_width = block_width(lab_count)
    fleet_width = block_width(fleet_count)
    lab_blocks = split_columns(lab_features, lab_width)
    fleet_blocks = split_columns(fleet_features, fleet_width)
    sq_lab_blocks = sq_lab.reshape(-1, lab_width)
    sq_fleet_blocks = sq_fleet.reshape(-1, fleet_width)
    log_b_blocks = log_b.reshape(-1, fleet_width)

    def update_lab(fleet_pot):
        def one_block(items):
            lab_part, sq_part = items
            score = (fleet_pot[None, :] - pair_cost(lab_part, sq_part, fleet_features, sq_fleet)) / EPS + log_b[None, :]
            top = jnp.max(score, axis=1)
            total = jnp.sum(jnp.exp(score - top[:, None]), axis=1)
            return -EPS * (top + jnp.log(total))
        return lax.map(one_block, (lab_blocks, sq_lab_blocks)).reshape(lab_count)

    def update_fleet(lab_pot):
        def one_block(items):
            fleet_part, sq_part = items
            score = (lab_pot[:, None] - pair_cost(lab_features, sq_lab, fleet_part, sq_part)) / EPS + log_a[:, None]
            top = jnp.max(score, axis=0)
            total = jnp.sum(jnp.exp(score - top[None, :]), axis=0)
            return -EPS * (top + jnp.log(total))
        return lax.map(one_block, (fleet_blocks, sq_fleet_blocks)).reshape(fleet_count)

    fleet_pot = jnp.zeros((fleet_count,), jnp.float32)
    lab_pot = jnp.zeros((lab_count,), jnp.float32)
    for step in range(ITERS):
        lab_pot = update_lab(fleet_pot)
        fleet_pot = update_fleet(lab_pot)

    fleet_pot_blocks = fleet_pot.reshape(-1, fleet_width)

    def gradient_block(items):
        fleet_part, sq_part, pot_part, log_part = items
        cost = pair_cost(lab_features, sq_lab, fleet_part, sq_part)
        plan = jnp.exp((lab_pot[:, None] + pot_part[None, :] - cost) / EPS + log_a[:, None] + log_part[None, :])
        mass = jnp.sum(plan, axis=0)
        weighted = jnp.dot(lab_float, plan, preferred_element_type=jnp.float32, precision=lax.Precision.HIGHEST)
        return 2.0 * (fleet_part.astype(jnp.float32) * mass[None, :] - weighted)

    pieces = lax.map(gradient_block, (fleet_blocks, sq_fleet_blocks, fleet_pot_blocks, log_b_blocks))
    fleet_gradient = pieces.transpose(1, 0, 2).reshape(fleet_features.shape[0], fleet_count)
    return lab_pot, fleet_pot, fleet_gradient
```

```python
import jax
import jax.numpy as jnp
from jax import lax
from jax.experimental import pallas as pl
from jax.experimental.pallas import tpu as pltpu
from jax.sharding import PartitionSpec as P


ITERS = 3
EPS = 0.5
LOG2E = 1.4426950408889634
LOW, HIGH = 2.0**-30, 2.0**60
LOW_RATIO, HIGH_RATIO = 2.0**-20, 2.0**20
MESH = pl.DeviceIdType.MESH
F32, BF16 = jnp.float32, jnp.bfloat16


def block_width():
    return 512


def split_columns(array, width):
    return array.reshape(array.shape[0], array.shape[1] // width, width).transpose(1, 0, 2)


def pair_cost(lab_part, sq_lab_part, fleet_part, sq_fleet_part):
    cross = lax.dot_general(
        lab_part, fleet_part, (((0,), (0,)), ((), ())), preferred_element_type=jnp.float32
    )
    return sq_lab_part[:, None] + sq_fleet_part[None, :] - 2.0 * cross


def square_sums(features):
    values = features.astype(jnp.float32)
    return jnp.sum(values * values, axis=0)


def reduce_over_fleet(top, total):
    whole_top = lax.pmax(top, "fleet")
    total = lax.psum(total * jnp.exp(top - whole_top), "fleet")
    top = whole_top
    return -EPS * (top + jnp.log(total))


def reduce_over_lab(top, total):
    whole_top = lax.pmax(top, "lab")
    total = lax.psum(total * jnp.exp(top - whole_top), "lab")
    top = whole_top
    return -EPS * (top + jnp.log(total))


def log_domain(lab_features, fleet_features, lab_weight, fleet_weight):
    lab_block = lax.all_gather(lab_features, "fleet", axis=1, tiled=True)
    fleet_block = lax.all_gather(fleet_features, "lab", axis=1, tiled=True)
    sq_lab = square_sums(lab_block)
    sq_fleet = square_sums(fleet_block)
    log_a = jnp.log(lab_weight)
    log_b = jnp.log(fleet_weight)
    lab_count = lab_block.shape[1]
    fleet_count = fleet_block.shape[1]
    lab_width = block_width()
    fleet_width = block_width()
    lab_blocks = split_columns(lab_block, lab_width)
    fleet_blocks = split_columns(fleet_block, fleet_width)
    sq_lab_blocks = sq_lab.reshape(-1, lab_width)
    sq_fleet_blocks = sq_fleet.reshape(-1, fleet_width)
    log_b_blocks = log_b.reshape(-1, fleet_width)

    def lab_partial(fleet_pot):

        def lab_one_block(items):
            lab_part, sq_part = items
            score = (
                fleet_pot[None, :] - pair_cost(lab_part, sq_part, fleet_block, sq_fleet)
            ) / EPS + log_b[None, :]
            top = jnp.max(score, axis=1)
            return (top, jnp.sum(jnp.exp(score - top[:, None]), axis=1))

        top, total = lax.map(lab_one_block, (lab_blocks, sq_lab_blocks))
        return (top.reshape(lab_count), total.reshape(lab_count))

    def fleet_partial(lab_pot):

        def fleet_one_block(items):
            fleet_part, sq_part = items
            score = (
                lab_pot[:, None] - pair_cost(lab_block, sq_lab, fleet_part, sq_part)
            ) / EPS + log_a[:, None]
            top = jnp.max(score, axis=0)
            return (top, jnp.sum(jnp.exp(score - top[None, :]), axis=0))

        top, total = lax.map(fleet_one_block, (fleet_blocks, sq_fleet_blocks))
        return (top.reshape(fleet_count), total.reshape(fleet_count))

    def iteration(step, pots):
        lab_top, lab_total = lab_partial(pots[1])
        lab_pot = reduce_over_fleet(lab_top, lab_total)
        fleet_top, fleet_total = fleet_partial(lab_pot)
        return (lab_pot, reduce_over_lab(fleet_top, fleet_total))

    lab_pot, fleet_pot = lax.fori_loop(
        0, ITERS, iteration, (jnp.zeros((lab_count,), F32), jnp.zeros((fleet_count,), F32))
    )
    pot_blocks = fleet_pot.reshape(-1, fleet_width)
    lab_float = lab_block.astype(jnp.float32)

    def gradient_block(items):
        fleet_part, sq_part, pot_part, log_part = items
        cost = pair_cost(lab_block, sq_lab, fleet_part, sq_part)
        plan = jnp.exp(
            (lab_pot[:, None] + pot_part[None, :] - cost) / EPS + log_a[:, None] + log_part[None, :]
        )
        mass = jnp.sum(plan, axis=0)
        weighted = jnp.dot(
            lab_float, plan, preferred_element_type=jnp.float32, precision=lax.Precision.HIGHEST
        )
        return 2.0 * (fleet_part.astype(jnp.float32) * mass[None, :] - weighted)

    pieces = lax.map(gradient_block, (fleet_blocks, sq_fleet_blocks, pot_blocks, log_b_blocks))
    terms = pieces.transpose(1, 0, 2).reshape(fleet_block.shape[0], fleet_count)
    fleet_gradient = lax.psum_scatter(terms, "lab", scatter_dimension=1, tiled=True)
    return (lab_pot, fleet_pot, fleet_gradient)


FEAT = 64
PIECE = 256
LAB_N, FLEET_N = 16, 8
LAB, FLEET = PIECE * FLEET_N, PIECE * LAB_N
LAB_T, FLEET_T = LAB // 128, FLEET // 128
ROWS = 512
LAB_OFFSETS = sorted(
    ((z, x) for z in range(4) for x in range(4) if (z, x) != (0, 0)),
    key=lambda o: -(min(o[0], 4 - o[0]) + min(o[1], 4 - o[1])),
)
FLEET_OFFSETS = (4, 5, 2, 3, 6, 7, 1)


def dot(left, right):
    return lax.dot_general(left, right, (((1,), (0,)), ((), ())), preferred_element_type=F32)


def kernel(
    x_ref, y_ref, a_ref, b_ref, f_ref, g_ref, grad_ref,
    xg, yg, xt, e_ref, lanes, spread, coef, sq_x, sq_y, scale, f_send, f_recv, g_send, g_recv, w_send, w_recv,
    x_ss, x_rs, y_ss, y_rs, f_ss, f_rs, g_ss, g_rs, w_ss, w_rs,
):
    me_l, me_f = lax.axis_index("lab"), lax.axis_index("fleet")
    fleet_peers = [lax.rem(me_f + d, FLEET_N) for d in FLEET_OFFSETS]
    lab_peers = [
        lax.rem(me_l // 4 + dz, 4) * 4 + lax.rem(lax.rem(me_l, 4) + dx, 4) for dz, dx in LAB_OFFSETS
    ]
    fleet_from = [lax.rem(me_f + FLEET_N - d, FLEET_N) for d in FLEET_OFFSETS]
    lab_from = [
        lax.rem(me_l // 4 + 4 - dz, 4) * 4 + lax.rem(lax.rem(me_l, 4) + 4 - dx, 4) for dz, dx in LAB_OFFSETS
    ]

    barrier = pltpu.get_barrier_semaphore()
    for p in lab_peers:
        pl.semaphore_signal(barrier, inc=1, device_id=(p, me_f), device_id_type=MESH)
    for p in fleet_peers:
        pl.semaphore_signal(barrier, inc=1, device_id=(me_l, p), device_id_type=MESH)
    pl.semaphore_wait(barrier, len(lab_peers) + len(fleet_peers))

    def copy_to_lab(n, src, dst, ss, rs):
        return pltpu.make_async_remote_copy(
            src_ref=src, dst_ref=dst, send_sem=ss.at[n], recv_sem=rs.at[n],
            device_id=(lab_peers[n], me_f), device_id_type=MESH,
        )

    def copy_to_fleet(n, src, dst, ss, rs):
        return pltpu.make_async_remote_copy(
            src_ref=src, dst_ref=dst, send_sem=ss.at[n], recv_sem=rs.at[n],
            device_id=(me_l, fleet_peers[n]), device_id_type=MESH,
        )

    copies = [copy_to_lab(n, y_ref, yg.at[me_l], y_ss, y_rs) for n in range(LAB_N - 1)]
    copies += [copy_to_fleet(n, x_ref, xg.at[me_f], x_ss, x_rs) for n in range(FLEET_N - 1)]
    for c in copies:
        c.start()
    xg[me_f] = x_ref[...]
    yg[me_l] = y_ref[...]
    for c in copies:
        c.wait()

    for p in range(FLEET_N):
        x = xg[p].astype(F32)
        xt[p * PIECE : (p + 1) * PIECE, :] = x.T.astype(BF16)
        sq = jnp.sum(x * x, axis=0, keepdims=True)
        sq_x[2 * p : 2 * p + 1, :] = sq[:, :128]
        sq_x[2 * p + 1 : 2 * p + 2, :] = sq[:, 128:]
    for p in range(LAB_N):
        y = yg[p].astype(F32)
        sq = jnp.sum(y * y, axis=0, keepdims=True)
        sq_y[2 * p : 2 * p + 1, :] = sq[:, :128]
        sq_y[2 * p + 1 : 2 * p + 2, :] = sq[:, 128:]
    scale[...] = b_ref[...] * jnp.exp2(sq_y[...] * (-LOG2E / EPS))

    def exp_rows(r, carry):
        rows = pl.ds(pl.multiple_of(r * ROWS, ROWS), ROWS)
        left = xt[rows, :]
        total = None
        for p in range(LAB_N):
            part = jnp.exp2(dot(left, yg[p]) * (2.0 * LOG2E / EPS))
            e_ref[rows, p * PIECE : (p + 1) * PIECE] = part
            for h in range(2):
                term = part[:, h * 128 : (h + 1) * 128] * scale[2 * p + h : 2 * p + h + 1, :]
                total = term if total is None else total + term
        lanes[rows, :] = total
        return carry

    lax.fori_loop(0, LAB // ROWS, exp_rows, 0)

    def lab_pass():
        beta = [jnp.broadcast_to(scale[t : t + 1, :], (8, 128)) for t in range(FLEET_T)]

        def rows_of(r, carry):
            for k in range(8):
                rows = pl.ds(pl.multiple_of(r * 64 + 8 * k, 8), 8)
                acc = [e_ref[rows, t * 128 : (t + 1) * 128] * beta[t] for t in range(4)]
                for t in range(4, FLEET_T):
                    acc[t % 4] = acc[t % 4] + e_ref[rows, t * 128 : (t + 1) * 128] * beta[t]
                lanes[rows, :] = (acc[0] + acc[1]) + (acc[2] + acc[3])
            return carry

        lax.fori_loop(0, LAB // 64, rows_of, 0)

    def lab_exchange(k, before):
        for t in range(LAB_T):
            f_send[k, t : t + 1, :] = jnp.sum(lanes[t * 128 : (t + 1) * 128, :].T, axis=0, keepdims=True)
        copies = [
            copy_to_fleet(n, f_send.at[k], f_recv.at[k, me_f], f_ss.at[k], f_rs.at[k]) for n in range(FLEET_N - 1)
        ]
        for c in copies:
            c.start()
        f_recv[k, me_f] = f_send[k]
        for c in copies:
            c.wait()
        total = f_recv[k, 0]
        for p in range(1, FLEET_N):
            total = total + f_recv[k, p]
        good = (total > LOW) & (total < HIGH)
        if before is not None:
            good = good & (total > before * LOW_RATIO) & (total < before * HIGH_RATIO)
        return jnp.where(good, total, jnp.nan)

    def fleet_pass():
        def rows_of(r, acc):
            rows = pl.ds(pl.multiple_of(r * 8, 8), 8)
            alpha = spread[rows, :]
            return tuple(acc[t] + e_ref[rows, t * 128 : (t + 1) * 128] * alpha for t in range(FLEET_T))

        acc = lax.fori_loop(
            0, LAB // 8, rows_of, tuple(jnp.zeros((8, 128), F32) for _ in range(FLEET_T)), unroll=8
        )
        return acc

    def fleet_exchange(k):
        copies = [
            copy_to_lab(n, g_send.at[k], g_recv.at[k, me_l], g_ss.at[k], g_rs.at[k]) for n in range(LAB_N - 1)
        ]
        for c in copies:
            c.start()
        g_recv[k, me_l] = g_send[k]
        for c in copies:
            c.wait()
        total = g_recv[k, 0]
        for p in range(1, LAB_N):
            total = total + g_recv[k, p]
        return total

    total_f = lab_exchange(0, None)
    for k in range(ITERS - 1):
        alpha = a_ref[...] / total_f
        for t in range(LAB_T):
            spread[t * 128 : (t + 1) * 128, :] = jnp.broadcast_to(alpha[t : t + 1, :], (128, 128)).T
        acc = fleet_pass()
        for t in range(FLEET_T):
            g_send[k, t : t + 1, :] = jnp.sum(acc[t], axis=0, keepdims=True)
        total_g = fleet_exchange(k)
        total_g = jnp.where((total_g > LOW) & (total_g < HIGH), total_g, jnp.nan)
        scale[...] = b_ref[...] / total_g
        lab_pass()
        total_f = lab_exchange(k + 1, total_f)

    f_ref[...] = sq_x[...] - EPS * jnp.log(total_f)

    alpha = a_ref[...] / total_f
    poison = jnp.sum(jnp.where(alpha == alpha, 0.0, 1.0))
    for t in range(LAB_T):
        cols = slice(t * 128, (t + 1) * 128)
        row = alpha[t : t + 1, :]
        x = xg[t // 2, :, (t % 2) * 128 : (t % 2 + 1) * 128].astype(F32) * row
        high = x.astype(BF16)
        coef[0:FEAT, cols] = high
        coef[FEAT : 2 * FEAT, cols] = (x - high.astype(F32)).astype(BF16)
        first = row.astype(BF16).astype(F32)
        second = (row - first).astype(BF16).astype(F32)
        third = row - first - second
        at = lax.broadcasted_iota(jnp.int32, (16, 128), 0)
        block = jnp.where(at == 0, first, jnp.where(at == 1, second, jnp.where(at == 2, third, 0.0)))
        coef[2 * FEAT : 2 * FEAT + 16, cols] = block.astype(BF16)

    left = coef[...]

    def columns(p):
        e = e_ref[:, pl.ds(pl.multiple_of(p * PIECE, PIECE), PIECE)]
        high = e.astype(BF16)
        out = dot(left, high) + dot(left, (e - high.astype(F32)).astype(BF16))
        weighted = out[:FEAT] + out[FEAT : 2 * FEAT]
        total = jnp.sum(out[2 * FEAT :], axis=0, keepdims=True)
        return weighted, jnp.where(poison > 0.0, jnp.nan, total)

    copies = []
    for n in range(LAB_N):
        p = lab_peers[n] if n < LAB_N - 1 else me_l
        weighted, total = columns(p)
        g_send[ITERS - 1, pl.ds(2 * p, 1), :] = total[:, :128]
        g_send[ITERS - 1, pl.ds(2 * p + 1, 1), :] = total[:, 128:]
        if n < LAB_N - 1:
            w_send[n] = weighted
            c = copy_to_lab(n, w_send.at[n], w_recv.at[n], w_ss, w_rs)
            c.start()
            copies.append(c)
        else:
            w_recv[n] = weighted
    total_g = fleet_exchange(ITERS - 1)
    g_ref[...] = sq_y[...] - EPS * jnp.log(total_g)
    scale[...] = total_g
    for c in copies:
        c.wait()
    weighted = w_recv[0]
    for n in range(1, LAB_N):
        weighted = weighted + w_recv[n]
    for h in range(2):
        cols = slice(h * 128, (h + 1) * 128)
        row = pl.ds(2 * me_l + h, 1)
        grad_ref[:, cols] = (2.0 * b_ref[row, :]) * (y_ref[:, cols].astype(F32) - weighted[:, cols] / scale[row, :])


def scaled(lab_features, fleet_features, lab_weight, fleet_weight):
    vmem = pl.BlockSpec(memory_space=pltpu.VMEM)
    dma = pltpu.SemaphoreType.DMA
    f, g, grad = pl.pallas_call(
        kernel,
        out_shape=[
            jax.ShapeDtypeStruct((LAB_T, 128), F32),
            jax.ShapeDtypeStruct((FLEET_T, 128), F32),
            jax.ShapeDtypeStruct((FEAT, PIECE), F32),
        ],
        in_specs=[vmem] * 4,
        out_specs=[vmem] * 3,
        scratch_shapes=[
            pltpu.VMEM((FLEET_N, FEAT, PIECE), BF16),
            pltpu.VMEM((LAB_N, FEAT, PIECE), BF16),
            pltpu.VMEM((LAB, FEAT), BF16),
            pltpu.VMEM((LAB, FLEET), F32),
            pltpu.VMEM((LAB, 128), F32),
            pltpu.VMEM((LAB, 128), F32),
            pltpu.VMEM((2 * FEAT + 16, LAB), BF16),
            pltpu.VMEM((LAB_T, 128), F32),
            pltpu.VMEM((FLEET_T, 128), F32),
            pltpu.VMEM((FLEET_T, 128), F32),
            pltpu.VMEM((ITERS, LAB_T, 128), F32),
            pltpu.VMEM((ITERS, FLEET_N, LAB_T, 128), F32),
            pltpu.VMEM((ITERS, FLEET_T, 128), F32),
            pltpu.VMEM((ITERS, LAB_N, FLEET_T, 128), F32),
            pltpu.VMEM((LAB_N - 1, FEAT, PIECE), F32),
            pltpu.VMEM((LAB_N, FEAT, PIECE), F32),
            dma((FLEET_N - 1,)),
            dma((FLEET_N - 1,)),
            dma((LAB_N - 1,)),
            dma((LAB_N - 1,)),
            dma((ITERS, FLEET_N - 1)),
            dma((ITERS, FLEET_N - 1)),
            dma((ITERS, LAB_N - 1)),
            dma((ITERS, LAB_N - 1)),
            dma((LAB_N - 1,)),
            dma((LAB_N - 1,)),
        ],
        name="sinkhorn",
        compiler_params=pltpu.CompilerParams(
            collective_id=0, has_side_effects=True, vmem_limit_bytes=56 * 2**20
        ),
    )(
        lab_features,
        fleet_features,
        lab_weight.reshape(LAB_T, 128),
        fleet_weight.reshape(FLEET_T, 128),
    )
    return f.reshape(LAB), g.reshape(FLEET), grad


def body(*args):
    outs = scaled(*args)
    return lax.cond(jnp.isnan(outs[1][0]), lambda: log_domain(*args), lambda: outs)


def solution(mesh):
    in_specs = (P(None, ("lab", "fleet")), P(None, ("fleet", "lab")), P("lab"), P("fleet"))
    out_specs = (P("lab"), P("fleet"), P(None, ("fleet", "lab")))
    return jax.shard_map(body, mesh=mesh, in_specs=in_specs, out_specs=out_specs, check_vma=False)
```

```python
import jax
import jax.numpy as jnp
from jax import lax
from jax.experimental import pallas as pl
from jax.experimental.pallas import tpu as pltpu
from jax.sharding import PartitionSpec as P


ITERS = 3
EPS = 0.5
LOG2E = 1.4426950408889634
LOW, HIGH = 2.0**-30, 2.0**60
LOW_RATIO, HIGH_RATIO = 2.0**-20, 2.0**20
MESH = pl.DeviceIdType.MESH
F32, BF16 = jnp.float32, jnp.bfloat16


def block_width():
    return 512


def split_columns(array, width):
    return array.reshape(array.shape[0], array.shape[1] // width, width).transpose(1, 0, 2)


def pair_cost(lab_part, sq_lab_part, fleet_part, sq_fleet_part):
    cross = lax.dot_general(
        lab_part, fleet_part, (((0,), (0,)), ((), ())), preferred_element_type=jnp.float32
    )
    return sq_lab_part[:, None] + sq_fleet_part[None, :] - 2.0 * cross


def square_sums(features):
    values = features.astype(jnp.float32)
    return jnp.sum(values * values, axis=0)


def ring(value, axis, visit, carry):
    n = lax.axis_size(axis)
    me = lax.axis_index(axis)

    right = [(i, (i + 1) % n) for i in range(n)]

    def step(k, state):
        block, carry = state
        carry = visit(lax.rem(me + n - k, n), block, carry)
        return lax.ppermute(block, axis, right), carry

    carry = visit(me, value, carry)
    return lax.fori_loop(1, n, step, (lax.ppermute(value, axis, right), carry))[1]


def gather(value, axis):
    def visit(index, block, out):
        return lax.dynamic_update_index_in_dim(out, block, index, 0)

    return ring(value, axis, visit, jnp.zeros((lax.axis_size(axis),) + value.shape, value.dtype))


def gather_columns(value, axis):
    return gather(value, axis).transpose(1, 0, 2).reshape(value.shape[0], -1)


def reduce_over(axis, top, total):
    tops, totals = gather(top, axis), gather(total, axis)
    top = jnp.max(tops, axis=0)
    total = jnp.sum(totals * jnp.exp(tops - top[None, :]), axis=0)
    return -EPS * (top + jnp.log(total))


def sum_own_columns(terms, axis):
    width = terms.shape[1] // lax.axis_size(axis)
    start = lax.axis_index(axis) * width

    def visit(index, block, out):
        return out + lax.dynamic_slice_in_dim(block, start, width, 1)

    return ring(terms, axis, visit, jnp.zeros((terms.shape[0], width), terms.dtype))


def log_domain(lab_features, fleet_features, lab_weight, fleet_weight):
    lab_block = gather_columns(lab_features, "fleet")
    fleet_block = gather_columns(fleet_features, "lab")
    sq_lab = square_sums(lab_block)
    sq_fleet = square_sums(fleet_block)
    log_a = jnp.log(lab_weight)
    log_b = jnp.log(fleet_weight)
    lab_count = lab_block.shape[1]
    fleet_count = fleet_block.shape[1]
    lab_width = block_width()
    fleet_width = block_width()
    lab_blocks = split_columns(lab_block, lab_width)
    fleet_blocks = split_columns(fleet_block, fleet_width)
    sq_lab_blocks = sq_lab.reshape(-1, lab_width)
    sq_fleet_blocks = sq_fleet.reshape(-1, fleet_width)
    log_b_blocks = log_b.reshape(-1, fleet_width)

    def lab_partial(fleet_pot):

        def lab_one_block(items):
            lab_part, sq_part = items
            score = (
                fleet_pot[None, :] - pair_cost(lab_part, sq_part, fleet_block, sq_fleet)
            ) / EPS + log_b[None, :]
            top = jnp.max(score, axis=1)
            return (top, jnp.sum(jnp.exp(score - top[:, None]), axis=1))

        top, total = lax.map(lab_one_block, (lab_blocks, sq_lab_blocks))
        return (top.reshape(lab_count), total.reshape(lab_count))

    def fleet_partial(lab_pot):

        def fleet_one_block(items):
            fleet_part, sq_part = items
            score = (
                lab_pot[:, None] - pair_cost(lab_block, sq_lab, fleet_part, sq_part)
            ) / EPS + log_a[:, None]
            top = jnp.max(score, axis=0)
            return (top, jnp.sum(jnp.exp(score - top[None, :]), axis=0))

        top, total = lax.map(fleet_one_block, (fleet_blocks, sq_fleet_blocks))
        return (top.reshape(fleet_count), total.reshape(fleet_count))

    def iteration(step, pots):
        lab_top, lab_total = lab_partial(pots[1])
        lab_pot = reduce_over("fleet", lab_top, lab_total)
        fleet_top, fleet_total = fleet_partial(lab_pot)
        return (lab_pot, reduce_over("lab", fleet_top, fleet_total))

    lab_pot, fleet_pot = lax.fori_loop(
        0, ITERS, iteration, (jnp.zeros((lab_count,), F32), jnp.zeros((fleet_count,), F32))
    )
    pot_blocks = fleet_pot.reshape(-1, fleet_width)
    lab_float = lab_block.astype(jnp.float32)

    def gradient_block(items):
        fleet_part, sq_part, pot_part, log_part = items
        cost = pair_cost(lab_block, sq_lab, fleet_part, sq_part)
        plan = jnp.exp(
            (lab_pot[:, None] + pot_part[None, :] - cost) / EPS + log_a[:, None] + log_part[None, :]
        )
        mass = jnp.sum(plan, axis=0)
        weighted = jnp.dot(
            lab_float, plan, preferred_element_type=jnp.float32, precision=lax.Precision.HIGHEST
        )
        return 2.0 * (fleet_part.astype(jnp.float32) * mass[None, :] - weighted)

    pieces = lax.map(gradient_block, (fleet_blocks, sq_fleet_blocks, pot_blocks, log_b_blocks))
    terms = pieces.transpose(1, 0, 2).reshape(fleet_block.shape[0], fleet_count)
    fleet_gradient = sum_own_columns(terms, "lab")
    return (lab_pot, fleet_pot, fleet_gradient)


FEAT = 64
PIECE = 256
LAB_N, FLEET_N = 16, 8
LAB, FLEET = PIECE * FLEET_N, PIECE * LAB_N
LAB_T, FLEET_T = LAB // 128, FLEET // 128
CHUNKS = 2
EXP_ROWS = 512
ROWS = LAB // CHUNKS
CHUNK_T = LAB_T // CHUNKS
WAVE = FLEET_N // 2


def hops(offset):
    return sum(min(d, 4 - d) for d in offset)


LAB_OFFSETS = sorted(((z, x) for z in range(4) for x in range(4) if (z, x) != (0, 0)), key=hops, reverse=True)
LAB_OWN = LAB_N - 1
FLEET_OFFSETS = (4, 2, 6, 1, 3, 5, 7)
Y_OFFSETS = (2, 1, 3)
EARLY = (LAB_OWN, 0, 1, 2, 3, 4)
LATER = tuple(n for n in range(LAB_N) if n not in EARLY)
GROUPS = ((0,), (1, 2), (3, 4, 5), (6, 7, 8, 9, 10), (11, 12, 13, 14, LAB_OWN))
LATE = 11


def owner_rows(position):
    piece = (position % WAVE) * 2 + position // WAVE
    return slice(2 * piece, 2 * piece + 2)


def dot(left, right):
    return lax.dot_general(left, right, (((1,), (0,)), ((), ())), preferred_element_type=F32)


def aligned(start, size, multiple):
    return pl.ds(pl.multiple_of(start, multiple), size)


def kernel(
    x_ref, y_ref, a_ref, b_ref, f_out, g_out, grad_out, flag_ref,
    xg, yg, xt, e_ref, lanes, spread, coef, sq_x, sq_y, scale, a_own, total_f, f_send, f_recv, g_send, g_recv,
    w_send, w_recv, f_ref, g_ref, grad_ref,
    x_rs, y_rs, f_rs, g_rs, w_rs, sent, out_s,
):
    me_l, me_f = lax.axis_index("lab"), lax.axis_index("fleet")
    core, chip = lax.rem(me_f, 2), me_f // 2

    def lab_at(dz, dx):
        return lax.rem(me_l // 4 + dz, 4) * 4 + lax.rem(lax.rem(me_l, 4) + dx, 4)

    fleet_to = [lax.rem(me_f + d, FLEET_N) for d in FLEET_OFFSETS]
    lab_to = [lab_at(dz, dx) for dz, dx in LAB_OFFSETS] + [me_l]
    lab_from = [lab_at(4 - dz, 4 - dx) for dz, dx in LAB_OFFSETS] + [me_l]

    barrier = pltpu.get_barrier_semaphore()
    for p in lab_to[:LAB_OWN]:
        pl.semaphore_signal(barrier, inc=1, device_id=(p, me_f), device_id_type=MESH)
    for p in fleet_to:
        pl.semaphore_signal(barrier, inc=1, device_id=(me_l, p), device_id_type=MESH)
    with jax.named_scope("barrier"):
        pl.semaphore_wait(barrier, LAB_N - 1 + FLEET_N - 1)

    def copy_to_lab(n, src, dst, send, recv):
        return pltpu.make_async_remote_copy(
            src_ref=src, dst_ref=dst, send_sem=send, recv_sem=recv,
            device_id=(lab_to[n], me_f), device_id_type=MESH,
        )

    def copy_to_fleet(to, src, dst, send, recv):
        return pltpu.make_async_remote_copy(
            src_ref=src, dst_ref=dst, send_sem=send, recv_sem=recv,
            device_id=(me_l, to), device_id_type=MESH,
        )

    def wait_sent(slots, send):
        copy_to_lab(0, slots, slots, sent.at[send], sent.at[send]).wait_send()

    def wait_received(slots, recv):
        copy_to_lab(0, slots, slots, sent.at[0], recv).wait_recv()

    sibling = chip * 2 + 1 - core
    mine = core * WAVE + chip
    x_copies = [
        copy_to_fleet(lax.rem(chip + d, 4) * 2 + core, x_ref, xg.at[mine], sent.at[0], x_rs.at[n])
        for n, d in enumerate(Y_OFFSETS)
    ]
    x_copies.append(copy_to_fleet(sibling, x_ref, xg.at[mine], sent.at[0], x_rs.at[3]))
    y_copies = [
        copy_to_lab(n, y_ref, yg.at[n], sent.at[1], y_rs.at[0 if n in EARLY else 1]) for n in range(LAB_N - 1)
    ]
    for c in x_copies + y_copies:
        c.start()
    xg[mine] = x_ref[...]
    yg[LAB_OWN] = y_ref[...]
    for at in range(FLEET_N):
        q, i = divmod(2 * at, CHUNK_T)
        a_own[q, i : i + 2, :] = a_ref[owner_rows(at), :]

    def x_prep(at):
        x = xg[at].astype(F32)
        xt[aligned(at * PIECE, PIECE, PIECE), :] = x.T.astype(BF16)
        sq = jnp.sum(x * x, axis=0, keepdims=True)
        for h in range(2):
            sq_x[pl.ds(2 * at + h, 1), :] = sq[:, h * 128 : (h + 1) * 128]

    def y_prep(n):
        y = yg[n].astype(F32)
        sq = jnp.sum(y * y, axis=0, keepdims=True)
        for h in range(2):
            row = pl.ds(2 * lab_from[n] + h, 1)
            part = sq[:, h * 128 : (h + 1) * 128]
            sq_y[row, :] = part
            scale[row, :] = b_ref[row, :] * jnp.exp2(part * (-LOG2E / EPS))

    def exp_rows(start, slots, first):
        rows = aligned(start, EXP_ROWS, EXP_ROWS)
        left = xt[rows, :]
        total = None if first else lanes[rows, :]
        for n in slots:
            part = jnp.exp2(dot(left, yg[n]) * (2.0 * LOG2E / EPS))
            e_ref[rows, aligned(lab_from[n] * PIECE, PIECE, PIECE)] = part
            for h in range(2):
                term = part[:, h * 128 : (h + 1) * 128] * scale[pl.ds(2 * lab_from[n] + h, 1), :]
                total = term if total is None else total + term
        lanes[rows, :] = total

    def copy_sums(k, q, n):
        return copy_to_fleet(fleet_to[n], f_send.at[k, q], f_recv.at[k, q, me_f], sent.at[2], f_rs.at[k, q])

    def send_sums(k, q):
        for t in range(CHUNK_T):
            rows = aligned(q * ROWS + t * 128, 128, 128)
            f_send[k, q, t : t + 1, :] = jnp.sum(lanes[rows, :].T, axis=0, keepdims=True)
        for n in range(FLEET_N - 1):
            copy_sums(k, q, n).start()
        f_recv[k, q, me_f] = f_send[k, q]

    y_prep(LAB_OWN)
    x_prep(mine)
    with jax.named_scope("x_wait"):
        for n, d in enumerate(Y_OFFSETS):
            x_copies[n].wait_recv()
            at = core * WAVE + lax.rem(chip + 4 - d, 4)
            copy_to_fleet(sibling, xg.at[at], xg.at[at], sent.at[0], x_rs.at[3]).start()
        for d in Y_OFFSETS:
            x_prep(core * WAVE + lax.rem(chip + 4 - d, 4))
    with jax.named_scope("y_far"):
        wait_received(yg.at[0 : len(EARLY) - 1], y_rs.at[0])
        for n in EARLY[1:]:
            y_prep(n)
    with jax.named_scope("exp_first"):
        for i in range(2):
            exp_rows(core * (LAB // 2) + i * EXP_ROWS, EARLY, True)
    with jax.named_scope("x_sibling"):
        wait_received(xg.at[0:WAVE], x_rs.at[3])
        for i in range(WAVE):
            x_prep((1 - core) * WAVE + i)
    with jax.named_scope("exp_second"):
        for i in range(2):
            exp_rows((1 - core) * (LAB // 2) + i * EXP_ROWS, EARLY, True)
    with jax.named_scope("y_near"):
        wait_received(yg.at[0 : len(LATER)], y_rs.at[1])
        for n in LATER:
            y_prep(n)

    def exp_chunk(q, carry):
        for i in range(ROWS // EXP_ROWS):
            exp_rows(q * ROWS + i * EXP_ROWS, LATER, False)
        send_sums(0, q)
        return carry

    with jax.named_scope("exp_rest"):
        lax.fori_loop(0, CHUNKS, exp_chunk, 0)

    def lab_pass(k):
        beta = [jnp.broadcast_to(scale[t : t + 1, :], (8, 128)) for t in range(FLEET_T)]

        def rows_of(r, carry):
            for i in range(8):
                rows = aligned(r * 64 + 8 * i, 8, 8)
                acc = [e_ref[rows, t * 128 : (t + 1) * 128] * beta[t] for t in range(4)]
                for t in range(4, FLEET_T):
                    acc[t % 4] = acc[t % 4] + e_ref[rows, t * 128 : (t + 1) * 128] * beta[t]
                lanes[rows, :] = (acc[0] + acc[1]) + (acc[2] + acc[3])
            return carry

        def chunk(q, carry):
            lax.fori_loop(q * (ROWS // 64), (q + 1) * (ROWS // 64), rows_of, 0)
            send_sums(k, q)
            return carry

        with jax.named_scope("lab_pass"):
            lax.fori_loop(0, CHUNKS, chunk, 0)

    def alpha_of(k, q):
        with jax.named_scope("lab_sums"):
            wait_received(f_recv.at[k, q, 0 : FLEET_N - 1], f_rs.at[k, q])
        total = f_recv[k, q, 0]
        for p in range(1, FLEET_N):
            total = total + f_recv[k, q, p]
        good = (total > LOW) & (total < HIGH)
        if k > 0:
            before = total_f[q]
            good = good & (total > before * LOW_RATIO) & (total < before * HIGH_RATIO)
        total = jnp.where(good, total, jnp.nan)
        total_f[q] = total
        return a_own[q] / total

    def fleet_pass(k):
        acc = tuple(jnp.zeros((8, 128), F32) for _ in range(FLEET_T))
        for q in range(CHUNKS):
            alpha = alpha_of(k, q)
            with jax.named_scope("fleet_pass"):
                for t in range(CHUNK_T):
                    rows = slice(q * ROWS + t * 128, q * ROWS + (t + 1) * 128)
                    spread[rows, :] = jnp.broadcast_to(alpha[t : t + 1, :], (128, 128)).T

                def rows_of(r, acc):
                    rows = aligned(r * 8, 8, 8)
                    factor = spread[rows, :]
                    return tuple(acc[t] + e_ref[rows, t * 128 : (t + 1) * 128] * factor for t in range(FLEET_T))

                acc = lax.fori_loop(q * (ROWS // 8), (q + 1) * (ROWS // 8), rows_of, acc, unroll=8)
        for t in range(FLEET_T):
            g_send[k, t : t + 1, :] = jnp.sum(acc[t], axis=0, keepdims=True)

    def start_fleet_sums(k):
        for n in range(LAB_N - 1):
            copy_to_lab(n, g_send.at[k], g_recv.at[k, me_l], sent.at[3], g_rs.at[k]).start()
        g_recv[k, me_l] = g_send[k]

    def end_fleet_sums(k):
        with jax.named_scope("fleet_sums"):
            wait_received(g_recv.at[k, 0 : LAB_N - 1], g_rs.at[k])
        total = g_recv[k, 0]
        for p in range(1, LAB_N):
            total = total + g_recv[k, p]
        return total

    for k in range(ITERS - 1):
        fleet_pass(k)
        start_fleet_sums(k)
        total = end_fleet_sums(k)
        total = jnp.where((total > LOW) & (total < HIGH), total, jnp.nan)
        scale[...] = b_ref[...] / total
        lab_pass(k + 1)

    lost = None
    for q in range(CHUNKS):
        alpha = alpha_of(ITERS - 1, q)
        potential = sq_x[q * CHUNK_T : (q + 1) * CHUNK_T, :] - EPS * jnp.log(total_f[q])
        for i in range(CHUNK_T // 2):
            f_ref[owner_rows(q * CHUNK_T // 2 + i), :] = potential[2 * i : 2 * i + 2]
        nans = jnp.where(alpha == alpha, 0.0, 1.0)
        lost = nans if lost is None else lost + nans
        for t in range(CHUNK_T):
            at = q * CHUNK_T + t
            cols = slice(at * 128, (at + 1) * 128)
            row = alpha[t : t + 1, :]
            x = xg[at // 2, :, (at % 2) * 128 : (at % 2 + 1) * 128].astype(F32) * row
            high = x.astype(BF16)
            coef[0:FEAT, cols] = high
            coef[FEAT : 2 * FEAT, cols] = (x - high.astype(F32)).astype(BF16)
            first = row.astype(BF16).astype(F32)
            second = (row - first).astype(BF16).astype(F32)
            third = row - first - second
            line = lax.broadcasted_iota(jnp.int32, (16, 128), 0)
            block = jnp.where(line == 0, first, jnp.where(line == 1, second, jnp.where(line == 2, third, 0.0)))
            coef[2 * FEAT : 2 * FEAT + 16, cols] = block.astype(BF16)

    outs = [pltpu.make_async_copy(src, dst, out_s.at[i]) for i, (src, dst) in enumerate(
        ((f_ref, f_out), (g_ref, g_out), (grad_ref, grad_out)))]
    outs[0].start()
    lost = jnp.sum(lost)
    left = coef[...]

    copies = [copy_to_lab(n, w_send.at[n], w_recv.at[n], sent.at[4], w_rs) for n in range(LAB_N - 1)]
    for group in GROUPS:
        with jax.named_scope("weighted"):
            for n in group:
                p = lab_to[n]
                e = e_ref[:, aligned(p * PIECE, PIECE, PIECE)]
                high = e.astype(BF16)
                out = dot(left, high) + dot(left, (e - high.astype(F32)).astype(BF16))
                weighted = out[:FEAT] + out[FEAT : 2 * FEAT]
                total = jnp.sum(out[2 * FEAT :], axis=0, keepdims=True)
                total = jnp.where(lost > 0.0, jnp.nan, total)
                for h in range(2):
                    g_send[ITERS - 1, pl.ds(2 * p + h, 1), :] = total[:, h * 128 : (h + 1) * 128]
                if n == LAB_OWN:
                    w_recv[n] = weighted
                else:
                    w_send[n] = weighted
            for n in group:
                if n < LATE:
                    copies[n].start()
    start_fleet_sums(ITERS - 1)
    for c in copies[LATE:]:
        c.start()
    total = end_fleet_sums(ITERS - 1)
    flag_ref[0] = jnp.where(jnp.sum(jnp.where(total == total, 0.0, 1.0)) > 0.0, 1, 0)
    g_ref[...] = sq_y[...] - EPS * jnp.log(total)
    outs[1].start()
    scale[...] = total
    with jax.named_scope("weighted_sums"):
        wait_received(w_recv.at[0 : LAB_N - 1], w_rs)
    weighted = w_recv[0]
    for n in range(1, LAB_N):
        weighted = weighted + w_recv[n]
    for h in range(2):
        cols = slice(h * 128, (h + 1) * 128)
        row = pl.ds(2 * me_l + h, 1)
        grad_ref[:, cols] = (2.0 * b_ref[row, :]) * (y_ref[:, cols].astype(F32) - weighted[:, cols] / scale[row, :])
    outs[2].start()
    with jax.named_scope("outputs"):
        wait_sent(xg.at[0 : FLEET_N - 1], 0)
        wait_sent(yg.at[0 : LAB_N - 1], 1)
        wait_sent(f_recv.at[:, :, 0 : FLEET_N - 1], 2)
        wait_sent(g_recv.at[:, 0 : LAB_N - 1], 3)
        wait_sent(w_recv.at[0 : LAB_N - 1], 4)
        for c in outs:
            c.wait()


OUT_SHAPES = [
    jax.ShapeDtypeStruct((LAB_T, 128), F32),
    jax.ShapeDtypeStruct((FLEET_T, 128), F32),
    jax.ShapeDtypeStruct((FEAT, PIECE), F32),
]


def copy_kernel(*refs):
    for i in range(3):
        refs[3 + i][...] = refs[i][...]


def copy_outs(*outs):
    vmem = pl.BlockSpec(memory_space=pltpu.VMEM)
    return pl.pallas_call(
        copy_kernel, out_shape=OUT_SHAPES, in_specs=[vmem] * 3, out_specs=[vmem] * 3, name="outputs"
    )(*outs)


def scaled(lab_features, fleet_features, lab_weight, fleet_weight):
    vmem = pl.BlockSpec(memory_space=pltpu.VMEM)
    anywhere = pl.BlockSpec(memory_space=pl.ANY)
    dma = pltpu.SemaphoreType.DMA
    return pl.pallas_call(
        kernel,
        out_shape=OUT_SHAPES + [jax.ShapeDtypeStruct((1,), jnp.int32)],
        in_specs=[vmem] * 4,
        out_specs=[anywhere] * 3 + [pl.BlockSpec(memory_space=pltpu.SMEM)],
        scratch_shapes=[
            pltpu.VMEM((FLEET_N, FEAT, PIECE), BF16),
            pltpu.VMEM((LAB_N, FEAT, PIECE), BF16),
            pltpu.VMEM((LAB, FEAT), BF16),
            pltpu.VMEM((LAB, FLEET), F32),
            pltpu.VMEM((LAB, 128), F32),
            pltpu.VMEM((LAB, 128), F32),
            pltpu.VMEM((2 * FEAT + 16, LAB), BF16),
            pltpu.VMEM((LAB_T, 128), F32),
            pltpu.VMEM((FLEET_T, 128), F32),
            pltpu.VMEM((FLEET_T, 128), F32),
            pltpu.VMEM((CHUNKS, CHUNK_T, 128), F32),
            pltpu.VMEM((CHUNKS, CHUNK_T, 128), F32),
            pltpu.VMEM((ITERS, CHUNKS, CHUNK_T, 128), F32),
            pltpu.VMEM((ITERS, CHUNKS, FLEET_N, CHUNK_T, 128), F32),
            pltpu.VMEM((ITERS, FLEET_T, 128), F32),
            pltpu.VMEM((ITERS, LAB_N, FLEET_T, 128), F32),
            pltpu.VMEM((LAB_N - 1, FEAT, PIECE), F32),
            pltpu.VMEM((LAB_N, FEAT, PIECE), F32),
            pltpu.VMEM((LAB_T, 128), F32),
            pltpu.VMEM((FLEET_T, 128), F32),
            pltpu.VMEM((FEAT, PIECE), F32),
            dma((4,)),
            dma((2,)),
            dma((ITERS, CHUNKS)),
            dma((ITERS,)),
            dma,
            dma((5,)),
            dma((3,)),
        ],
        name="sinkhorn",
        compiler_params=pltpu.CompilerParams(
            collective_id=0, has_side_effects=True, vmem_limit_bytes=56 * 2**20
        ),
    )(
        lab_features,
        fleet_features,
        lab_weight.reshape(LAB_T, 128),
        fleet_weight.reshape(FLEET_T, 128),
    )


def body(*args):
    *outs, flag = scaled(*args)

    def general():
        f, g, grad = log_domain(*args)
        return [f.reshape(LAB_T, 128), g.reshape(FLEET_T, 128), grad]

    f, g, grad = copy_outs(*lax.cond(flag[0] != 0, general, lambda: outs))
    return f.reshape(LAB), g.reshape(FLEET), grad


def solution(mesh):
    in_specs = (P(None, ("lab", "fleet")), P(None, ("fleet", "lab")), P("lab"), P("fleet"))
    out_specs = (P("lab"), P("fleet"), P(None, ("fleet", "lab")))
    return jax.shard_map(body, mesh=mesh, in_specs=in_specs, out_specs=out_specs, check_vma=False)
```

```python
import jax
import jax.numpy as jnp
from jax import lax
from jax.experimental import pallas as pl
from jax.experimental.pallas import tpu as pltpu
from jax.sharding import PartitionSpec as P


ITERS = 3
EPS = 0.5
LOG2E = 1.4426950408889634
LOW, HIGH = 2.0**-30, 2.0**60
LOW_RATIO, HIGH_RATIO = 2.0**-20, 2.0**20
MESH = pl.DeviceIdType.MESH
F32, BF16 = jnp.float32, jnp.bfloat16


def block_width():
    return 512


def split_columns(array, width):
    return array.reshape(array.shape[0], array.shape[1] // width, width).transpose(1, 0, 2)


def pair_cost(lab_part, sq_lab_part, fleet_part, sq_fleet_part):
    cross = lax.dot_general(
        lab_part, fleet_part, (((0,), (0,)), ((), ())), preferred_element_type=jnp.float32
    )
    return sq_lab_part[:, None] + sq_fleet_part[None, :] - 2.0 * cross


def square_sums(features):
    values = features.astype(jnp.float32)
    return jnp.sum(values * values, axis=0)


def ring(value, axis, visit, carry):
    n = lax.axis_size(axis)
    me = lax.axis_index(axis)

    right = [(i, (i + 1) % n) for i in range(n)]

    def step(k, state):
        block, carry = state
        carry = visit(lax.rem(me + n - k, n), block, carry)
        return lax.ppermute(block, axis, right), carry

    carry = visit(me, value, carry)
    return lax.fori_loop(1, n, step, (lax.ppermute(value, axis, right), carry))[1]


def gather(value, axis):
    def visit(index, block, out):
        return lax.dynamic_update_index_in_dim(out, block, index, 0)

    return ring(value, axis, visit, jnp.zeros((lax.axis_size(axis),) + value.shape, value.dtype))


def gather_columns(value, axis):
    return gather(value, axis).transpose(1, 0, 2).reshape(value.shape[0], -1)


def reduce_over(axis, top, total):
    tops, totals = gather(top, axis), gather(total, axis)
    top = jnp.max(tops, axis=0)
    total = jnp.sum(totals * jnp.exp(tops - top[None, :]), axis=0)
    return -EPS * (top + jnp.log(total))


def sum_own_columns(terms, axis):
    width = terms.shape[1] // lax.axis_size(axis)
    start = lax.axis_index(axis) * width

    def visit(index, block, out):
        return out + lax.dynamic_slice_in_dim(block, start, width, 1)

    return ring(terms, axis, visit, jnp.zeros((terms.shape[0], width), terms.dtype))


def log_domain(lab_features, fleet_features, lab_weight, fleet_weight):
    lab_block = gather_columns(lab_features, "fleet")
    fleet_block = gather_columns(fleet_features, "lab")
    sq_lab = square_sums(lab_block)
    sq_fleet = square_sums(fleet_block)
    log_a = jnp.log(lab_weight)
    log_b = jnp.log(fleet_weight)
    lab_count = lab_block.shape[1]
    fleet_count = fleet_block.shape[1]
    lab_width = block_width()
    fleet_width = block_width()
    lab_blocks = split_columns(lab_block, lab_width)
    fleet_blocks = split_columns(fleet_block, fleet_width)
    sq_lab_blocks = sq_lab.reshape(-1, lab_width)
    sq_fleet_blocks = sq_fleet.reshape(-1, fleet_width)
    log_b_blocks = log_b.reshape(-1, fleet_width)

    def lab_partial(fleet_pot):

        def lab_one_block(items):
            lab_part, sq_part = items
            score = (
                fleet_pot[None, :] - pair_cost(lab_part, sq_part, fleet_block, sq_fleet)
            ) / EPS + log_b[None, :]
            top = jnp.max(score, axis=1)
            return (top, jnp.sum(jnp.exp(score - top[:, None]), axis=1))

        top, total = lax.map(lab_one_block, (lab_blocks, sq_lab_blocks))
        return (top.reshape(lab_count), total.reshape(lab_count))

    def fleet_partial(lab_pot):

        def fleet_one_block(items):
            fleet_part, sq_part = items
            score = (
                lab_pot[:, None] - pair_cost(lab_block, sq_lab, fleet_part, sq_part)
            ) / EPS + log_a[:, None]
            top = jnp.max(score, axis=0)
            return (top, jnp.sum(jnp.exp(score - top[None, :]), axis=0))

        top, total = lax.map(fleet_one_block, (fleet_blocks, sq_fleet_blocks))
        return (top.reshape(fleet_count), total.reshape(fleet_count))

    def iteration(step, pots):
        lab_top, lab_total = lab_partial(pots[1])
        lab_pot = reduce_over("fleet", lab_top, lab_total)
        fleet_top, fleet_total = fleet_partial(lab_pot)
        return (lab_pot, reduce_over("lab", fleet_top, fleet_total))

    lab_pot, fleet_pot = lax.fori_loop(
        0, ITERS, iteration, (jnp.zeros((lab_count,), F32), jnp.zeros((fleet_count,), F32))
    )
    pot_blocks = fleet_pot.reshape(-1, fleet_width)
    lab_float = lab_block.astype(jnp.float32)

    def gradient_block(items):
        fleet_part, sq_part, pot_part, log_part = items
        cost = pair_cost(lab_block, sq_lab, fleet_part, sq_part)
        plan = jnp.exp(
            (lab_pot[:, None] + pot_part[None, :] - cost) / EPS + log_a[:, None] + log_part[None, :]
        )
        mass = jnp.sum(plan, axis=0)
        weighted = jnp.dot(
            lab_float, plan, preferred_element_type=jnp.float32, precision=lax.Precision.HIGHEST
        )
        return 2.0 * (fleet_part.astype(jnp.float32) * mass[None, :] - weighted)

    pieces = lax.map(gradient_block, (fleet_blocks, sq_fleet_blocks, pot_blocks, log_b_blocks))
    terms = pieces.transpose(1, 0, 2).reshape(fleet_block.shape[0], fleet_count)
    fleet_gradient = sum_own_columns(terms, "lab")
    return (lab_pot, fleet_pot, fleet_gradient)


FEAT = 64
PIECE = 256
LAB_N, FLEET_N = 16, 8
LAB, FLEET = PIECE * FLEET_N, PIECE * LAB_N
LAB_T, FLEET_T = LAB // 128, FLEET // 128
CHUNKS = 4
EXP_ROWS = 1024
TOGETHER = (2, 1, 2)
HALF = FEAT // 2
ROWS = LAB // CHUNKS
CHUNK_T = LAB_T // CHUNKS
WAVE = FLEET_N // 2


def hops(offset):
    return sum(min(d, 4 - d) for d in offset)


LAB_OFFSETS = sorted(((z, x) for z in range(4) for x in range(4) if (z, x) != (0, 0)), key=hops)
LAB_OWN = LAB_N - 1
FLEET_OFFSETS = (4, 2, 6, 1, 3, 5, 7)
Y_OFFSETS = (2, 1, 3)
NEAR, MIDDLE, FAR = (LAB_OWN, 0, 1, 2, 3), (4, 5, 6, 7, 8, 9), (10, 11, 12, 13, 14)
GROUPS = (
    ((2, 2), (2, 1)),
    ((2, 3), (1, 2), (3, 2)),
    ((1, 1), (1, 3), (3, 1), (3, 3)),
    ((0, 2), (2, 0), (0, 1), (1, 0)),
    ((0, 3), (3, 0), (0, 0)),
)
DEPTH = 256


def owner_rows(position):
    piece = (position % WAVE) * 2 + position // WAVE
    return slice(2 * piece, 2 * piece + 2)


def dot(left, right):
    return lax.dot_general(left, right, (((1,), (0,)), ((), ())), preferred_element_type=F32)


def aligned(start, size, multiple):
    return pl.ds(pl.multiple_of(start, multiple), size)


def kernel(
    x_ref, y_ref, a_ref, b_ref, f_out, g_out, grad_out, flag_ref,
    xg, yg, xt, e_ref, lanes, spread, coef, sq_x, sq_y, scale, a_own, total_f, f_send, f_recv, g_send, g_recv,
    w_send, wx, wz, wx_sum, wz_sum, wxz, wzx, f_ref, g_ref, grad_ref,
    x_rs, y_rs, f_rs, g_rs, wx_rs, wz_rs, w_rs, sent, out_s,
):
    me_l, me_f = lax.axis_index("lab"), lax.axis_index("fleet")
    core, chip = lax.rem(me_f, 2), me_f // 2
    me_z, me_x = me_l // 4, lax.rem(me_l, 4)

    def lab_at(dz, dx):
        return lax.rem(me_z + dz, 4) * 4 + lax.rem(me_x + dx, 4)

    fleet_to = [lax.rem(me_f + d, FLEET_N) for d in FLEET_OFFSETS]
    lab_to = [lab_at(dz, dx) for dz, dx in LAB_OFFSETS] + [me_l]
    lab_from = [lab_at(4 - dz, 4 - dx) for dz, dx in LAB_OFFSETS] + [me_l]

    barrier = pltpu.get_barrier_semaphore()
    for p in reversed(lab_to[:LAB_OWN]):
        pl.semaphore_signal(barrier, inc=1, device_id=(p, me_f), device_id_type=MESH)
    for p in fleet_to:
        pl.semaphore_signal(barrier, inc=1, device_id=(me_l, p), device_id_type=MESH)
    with jax.named_scope("barrier"):
        pl.semaphore_wait(barrier, LAB_N - 1 + FLEET_N - 1)

    def copy_to_lab(n, src, dst, send, recv):
        return pltpu.make_async_remote_copy(
            src_ref=src, dst_ref=dst, send_sem=send, recv_sem=recv,
            device_id=(lab_to[n], me_f), device_id_type=MESH,
        )

    def copy_to_offset(dz, dx, src, dst, send, recv):
        return pltpu.make_async_remote_copy(
            src_ref=src, dst_ref=dst, send_sem=sent.at[send], recv_sem=recv,
            device_id=(lab_at(dz, dx), me_f), device_id_type=MESH,
        )

    def copy_to_fleet(to, src, dst, send, recv):
        return pltpu.make_async_remote_copy(
            src_ref=src, dst_ref=dst, send_sem=send, recv_sem=recv,
            device_id=(me_l, to), device_id_type=MESH,
        )

    def wait_sent(slots, send):
        copy_to_lab(0, slots, slots, sent.at[send], sent.at[send]).wait_send()

    def wait_received(slots, recv):
        copy_to_lab(0, slots, slots, sent.at[0], recv).wait_recv()

    sibling = chip * 2 + 1 - core
    mine = core * WAVE + chip
    x_copies = [
        copy_to_fleet(lax.rem(chip + d, 4) * 2 + core, x_ref, xg.at[mine], sent.at[0], x_rs.at[n])
        for n, d in enumerate(Y_OFFSETS)
    ]
    x_copies.append(copy_to_fleet(sibling, x_ref, xg.at[mine], sent.at[0], x_rs.at[3]))
    y_copies = [
        copy_to_lab(n, y_ref, yg.at[n], sent.at[1], y_rs.at[0 if n in NEAR else 1 if n in MIDDLE else 2]) for n in range(LAB_N - 1)
    ]
    for c in x_copies + y_copies:
        c.start()
    xg[mine] = x_ref[...]
    yg[LAB_OWN] = y_ref[...]
    for at in range(FLEET_N):
        q, i = divmod(2 * at, CHUNK_T)
        a_own[q, i : i + 2, :] = a_ref[owner_rows(at), :]

    def x_prep(at):
        x = xg[at].astype(F32)
        xt[aligned(at * PIECE, PIECE, PIECE), :] = x.T.astype(BF16)
        sq = jnp.sum(x * x, axis=0, keepdims=True)
        for h in range(2):
            sq_x[pl.ds(2 * at + h, 1), :] = sq[:, h * 128 : (h + 1) * 128]

    def y_prep(n):
        y = yg[n].astype(F32)
        sq = jnp.sum(y * y, axis=0, keepdims=True)
        for h in range(2):
            row = pl.ds(2 * lab_from[n] + h, 1)
            part = sq[:, h * 128 : (h + 1) * 128]
            sq_y[row, :] = part
            scale[row, :] = b_ref[row, :] * jnp.exp2(part * (-LOG2E / EPS))

    def exp_rows(start, slots, first):
        rows = aligned(start, EXP_ROWS, EXP_ROWS)
        left = xt[rows, :]
        total = None if first else lanes[rows, :]
        for n in slots:
            part = jnp.exp2(dot(left, yg[n]) * (2.0 * LOG2E / EPS))
            e_ref[rows, aligned(lab_from[n] * PIECE, PIECE, PIECE)] = part
            for h in range(2):
                term = part[:, h * 128 : (h + 1) * 128] * scale[pl.ds(2 * lab_from[n] + h, 1), :]
                total = term if total is None else total + term
        lanes[rows, :] = total

    def copy_sums(k, q, n):
        chunks = pl.ds(q, TOGETHER[k])
        return copy_to_fleet(
            fleet_to[n], f_send.at[k, chunks], f_recv.at[k, me_f, chunks], sent.at[2], f_rs.at[k, q]
        )

    def send_sums(k, q):
        for t in range(CHUNK_T * TOGETHER[k]):
            rows = aligned(q * ROWS + t * 128, 128, 128)
            part = jnp.sum(lanes[rows, :].T, axis=0, keepdims=True)
            f_send[k, q + t // CHUNK_T, t % CHUNK_T : t % CHUNK_T + 1, :] = part
        for n in range(FLEET_N - 1):
            copy_sums(k, q, n).start()
        for i in range(TOGETHER[k]):
            f_recv[k, me_f, q + i] = f_send[k, q + i]

    y_prep(LAB_OWN)
    x_prep(mine)
    with jax.named_scope("x_wait"):
        for n, d in enumerate(Y_OFFSETS):
            x_copies[n].wait_recv()
            at = core * WAVE + lax.rem(chip + 4 - d, 4)
            copy_to_fleet(sibling, xg.at[at], xg.at[at], sent.at[0], x_rs.at[3]).start()
        for d in Y_OFFSETS:
            x_prep(core * WAVE + lax.rem(chip + 4 - d, 4))
    with jax.named_scope("y_near"):
        wait_received(yg.at[0 : len(NEAR) - 1], y_rs.at[0])
        for n in NEAR[1:]:
            y_prep(n)
    with jax.named_scope("exp_first"):
        exp_rows(core * EXP_ROWS, NEAR, True)
    with jax.named_scope("x_sibling"):
        wait_received(xg.at[0:WAVE], x_rs.at[3])
        for i in range(WAVE):
            x_prep((1 - core) * WAVE + i)
    with jax.named_scope("exp_second"):
        exp_rows((1 - core) * EXP_ROWS, NEAR, True)
    with jax.named_scope("y_middle"):
        wait_received(yg.at[0 : len(MIDDLE)], y_rs.at[1])
        for n in MIDDLE:
            y_prep(n)

    def exp_middle(i, carry):
        exp_rows(i * EXP_ROWS, MIDDLE, False)
        return carry

    with jax.named_scope("exp_middle"):
        lax.fori_loop(0, LAB // EXP_ROWS, exp_middle, 0)
    with jax.named_scope("y_far"):
        wait_received(yg.at[0 : len(FAR)], y_rs.at[2])
        for n in FAR:
            y_prep(n)

    def exp_far(i, carry):
        exp_rows(i * EXP_ROWS, FAR, False)
        send_sums(0, i * TOGETHER[0])
        return carry

    with jax.named_scope("exp_far"):
        lax.fori_loop(0, LAB // EXP_ROWS, exp_far, 0)

    def lab_pass(k):
        beta = [jnp.broadcast_to(scale[t : t + 1, :], (8, 128)) for t in range(FLEET_T)]

        def rows_of(r, carry):
            for i in range(8):
                rows = aligned(r * 64 + 8 * i, 8, 8)
                acc = [e_ref[rows, t * 128 : (t + 1) * 128] * beta[t] for t in range(4)]
                for t in range(4, FLEET_T):
                    acc[t % 4] = acc[t % 4] + e_ref[rows, t * 128 : (t + 1) * 128] * beta[t]
                lanes[rows, :] = (acc[0] + acc[1]) + (acc[2] + acc[3])
            return carry

        steps = TOGETHER[k] * ROWS // 64

        def chunks(i, carry):
            lax.fori_loop(i * steps, (i + 1) * steps, rows_of, 0)
            send_sums(k, i * TOGETHER[k])
            return carry

        with jax.named_scope("lab_pass"):
            lax.fori_loop(0, CHUNKS // TOGETHER[k], chunks, 0)

    def alpha_of(k, q):
        if q % TOGETHER[k] == 0:
            with jax.named_scope("lab_sums"):
                wait_received(f_recv.at[k, 0 : FLEET_N - 1, q : q + TOGETHER[k]], f_rs.at[k, q])
        total = f_recv[k, 0, q]
        for p in range(1, FLEET_N):
            total = total + f_recv[k, p, q]
        good = (total > LOW) & (total < HIGH)
        if k > 0:
            before = total_f[q]
            good = good & (total > before * LOW_RATIO) & (total < before * HIGH_RATIO)
        total = jnp.where(good, total, jnp.nan)
        total_f[q] = total
        return a_own[q] / total

    def fleet_pass(k):
        acc = tuple(jnp.zeros((8, 128), F32) for _ in range(FLEET_T))
        for q in range(CHUNKS):
            alpha = alpha_of(k, q)
            with jax.named_scope("fleet_pass"):
                for t in range(CHUNK_T):
                    rows = slice(q * ROWS + t * 128, q * ROWS + (t + 1) * 128)
                    spread[rows, :] = jnp.broadcast_to(alpha[t : t + 1, :], (128, 128)).T

                def rows_of(r, acc):
                    rows = aligned(r * 8, 8, 8)
                    factor = spread[rows, :]
                    return tuple(acc[t] + e_ref[rows, t * 128 : (t + 1) * 128] * factor for t in range(FLEET_T))

                acc = lax.fori_loop(q * (ROWS // 8), (q + 1) * (ROWS // 8), rows_of, acc, unroll=8)
        for t in range(FLEET_T):
            g_send[k, t : t + 1, :] = jnp.sum(acc[t], axis=0, keepdims=True)

    def start_fleet_sums(k):
        for n in reversed(range(LAB_N - 1)):
            copy_to_lab(n, g_send.at[k], g_recv.at[k, me_l], sent.at[3], g_rs.at[k]).start()
        g_recv[k, me_l] = g_send[k]

    def end_fleet_sums(k):
        with jax.named_scope("fleet_sums"):
            wait_received(g_recv.at[k, 0 : LAB_N - 1], g_rs.at[k])
        total = g_recv[k, 0]
        for p in range(1, LAB_N):
            total = total + g_recv[k, p]
        return total

    for k in range(ITERS - 1):
        fleet_pass(k)
        start_fleet_sums(k)
        total = end_fleet_sums(k)
        total = jnp.where((total > LOW) & (total < HIGH), total, jnp.nan)
        scale[...] = b_ref[...] / total
        lab_pass(k + 1)

    lost = None
    for q in range(CHUNKS):
        alpha = alpha_of(ITERS - 1, q)
        potential = sq_x[q * CHUNK_T : (q + 1) * CHUNK_T, :] - EPS * jnp.log(total_f[q])
        for i in range(CHUNK_T // 2):
            f_ref[owner_rows(q * CHUNK_T // 2 + i), :] = potential[2 * i : 2 * i + 2]
        nans = jnp.where(alpha == alpha, 0.0, 1.0)
        lost = nans if lost is None else lost + nans
        for t in range(CHUNK_T):
            at = q * CHUNK_T + t
            cols = slice(at * 128, (at + 1) * 128)
            row = alpha[t : t + 1, :]
            x = xg[at // 2, :, (at % 2) * 128 : (at % 2 + 1) * 128].astype(F32) * row
            high = x.astype(BF16)
            coef[0:FEAT, cols] = high
            coef[FEAT : 2 * FEAT, cols] = (x - high.astype(F32)).astype(BF16)
            first = row.astype(BF16).astype(F32)
            second = (row - first).astype(BF16).astype(F32)
            third = row - first - second
            line = lax.broadcasted_iota(jnp.int32, (16, 128), 0)
            block = jnp.where(line == 0, first, jnp.where(line == 1, second, jnp.where(line == 2, third, 0.0)))
            coef[2 * FEAT : 2 * FEAT + 16, cols] = block.astype(BF16)

    outs = [pltpu.make_async_copy(src, dst, out_s.at[i]) for i, (src, dst) in enumerate(
        ((f_ref, f_out), (g_ref, g_out), (grad_ref, grad_out)))]
    outs[0].start()
    lost = jnp.sum(lost)

    for group in GROUPS:
        with jax.named_scope("weighted"):
            for dz, dx in group:
                p, at = lab_at(dz, dx), dz * 4 + dx
                cols = aligned(p * PIECE, PIECE, PIECE)
                part = None
                for k in range(LAB // DEPTH):
                    rows = slice(k * DEPTH, (k + 1) * DEPTH)
                    e, left = e_ref[rows, cols], coef[:, rows]
                    high = e.astype(BF16)
                    term = dot(left, high) + dot(left, (e - high.astype(F32)).astype(BF16))
                    part = term if part is None else part + term
                weighted = part[:FEAT] + part[FEAT : 2 * FEAT]
                total = jnp.sum(part[2 * FEAT :], axis=0, keepdims=True)
                total = jnp.where(lost > 0.0, jnp.nan, total)
                for h in range(2):
                    g_send[ITERS - 1, pl.ds(2 * p + h, 1), :] = total[:, h * 128 : (h + 1) * 128]
                if dx == 0:
                    wx[3, dz] = weighted[:HALF]
                if dz == 0:
                    wz[3, dx] = weighted[HALF:]
                w_send[at] = weighted
            for dz, dx in group:
                at = dz * 4 + dx
                if dx != 0:
                    copy_to_offset(0, dx, w_send.at[at, 0:HALF], wx.at[dx - 1, dz], 4, wx_rs.at[dz]).start()
                if dz != 0:
                    copy_to_offset(dz, 0, w_send.at[at, HALF:FEAT], wz.at[dz - 1, dx], 5, wz_rs.at[dx]).start()

    start_fleet_sums(ITERS - 1)

    def sum_of(parts):
        return (parts[0] + parts[1]) + (parts[2] + parts[3])

    with jax.named_scope("weighted_first"):
        for d in (2, 1, 3):
            wait_received(wx.at[0:3, d], wx_rs.at[d])
            wx_sum[d - 1] = sum_of([wx[i, d] for i in range(4)])
            copy_to_offset(d, 0, wx_sum.at[d - 1], wxz.at[d - 1], 6, w_rs.at[0]).start()
            wait_received(wz.at[0:3, d], wz_rs.at[d])
            wz_sum[d - 1] = sum_of([wz[i, d] for i in range(4)])
            copy_to_offset(0, d, wz_sum.at[d - 1], wzx.at[d - 1], 7, w_rs.at[1]).start()
    wait_received(wx.at[0:3, 0], wx_rs.at[0])
    wait_received(wz.at[0:3, 0], wz_rs.at[0])
    upper = sum_of([wx[i, 0] for i in range(4)])
    lower = sum_of([wz[i, 0] for i in range(4)])
    total = end_fleet_sums(ITERS - 1)
    scale[...] = total
    flag_ref[0] = jnp.where(jnp.sum(jnp.where(total == total, 0.0, 1.0)) > 0.0, 1, 0)
    g_ref[...] = sq_y[...] - EPS * jnp.log(total)
    outs[1].start()
    with jax.named_scope("weighted_second"):
        wait_received(wxz.at[0:3], w_rs.at[0])
        wait_received(wzx.at[0:3], w_rs.at[1])
    upper = sum_of([upper] + [wxz[i] for i in range(3)])
    lower = sum_of([lower] + [wzx[i] for i in range(3)])
    for h in range(2):
        cols = slice(h * 128, (h + 1) * 128)
        row = pl.ds(2 * me_l + h, 1)
        factor, inverse = 2.0 * b_ref[row, :], 1.0 / scale[row, :]
        for part, rows in ((upper, slice(0, HALF)), (lower, slice(HALF, FEAT))):
            grad_ref[rows, cols] = factor * (y_ref[rows, cols].astype(F32) - part[:, cols] * inverse)
    outs[2].start()
    with jax.named_scope("outputs"):
        wait_sent(xg.at[0 : FLEET_N - 1], 0)
        wait_sent(yg.at[0 : LAB_N - 1], 1)
        wait_sent(f_recv.at[:, 0 : FLEET_N - 1], 2)
        wait_sent(g_recv.at[:, 0 : LAB_N - 1], 3)
        for i, slots in enumerate((wx, wz, wxz, wzx)):
            wait_sent(slots.at[0:3], 4 + i)
        for c in outs:
            c.wait()


OUT_SHAPES = [
    jax.ShapeDtypeStruct((LAB_T, 128), F32),
    jax.ShapeDtypeStruct((FLEET_T, 128), F32),
    jax.ShapeDtypeStruct((FEAT, PIECE), F32),
]


def copy_kernel(*refs):
    for i in range(3):
        refs[3 + i][...] = refs[i][...]


def copy_outs(*outs):
    vmem = pl.BlockSpec(memory_space=pltpu.VMEM)
    return pl.pallas_call(
        copy_kernel, out_shape=OUT_SHAPES, in_specs=[vmem] * 3, out_specs=[vmem] * 3, name="outputs"
    )(*outs)


def scaled(lab_features, fleet_features, lab_weight, fleet_weight):
    vmem = pl.BlockSpec(memory_space=pltpu.VMEM)
    anywhere = pl.BlockSpec(memory_space=pl.ANY)
    dma = pltpu.SemaphoreType.DMA
    return pl.pallas_call(
        kernel,
        out_shape=OUT_SHAPES + [jax.ShapeDtypeStruct((1,), jnp.int32)],
        in_specs=[vmem] * 4,
        out_specs=[anywhere] * 3 + [pl.BlockSpec(memory_space=pltpu.SMEM)],
        scratch_shapes=[
            pltpu.VMEM((FLEET_N, FEAT, PIECE), BF16),
            pltpu.VMEM((LAB_N, FEAT, PIECE), BF16),
            pltpu.VMEM((LAB, FEAT), BF16),
            pltpu.VMEM((LAB, FLEET), F32),
            pltpu.VMEM((LAB, 128), F32),
            pltpu.VMEM((LAB, 128), F32),
            pltpu.VMEM((2 * FEAT + 16, LAB), BF16),
            pltpu.VMEM((LAB_T, 128), F32),
            pltpu.VMEM((FLEET_T, 128), F32),
            pltpu.VMEM((FLEET_T, 128), F32),
            pltpu.VMEM((CHUNKS, CHUNK_T, 128), F32),
            pltpu.VMEM((CHUNKS, CHUNK_T, 128), F32),
            pltpu.VMEM((ITERS, CHUNKS, CHUNK_T, 128), F32),
            pltpu.VMEM((ITERS, FLEET_N, CHUNKS, CHUNK_T, 128), F32),
            pltpu.VMEM((ITERS, FLEET_T, 128), F32),
            pltpu.VMEM((ITERS, LAB_N, FLEET_T, 128), F32),
            pltpu.VMEM((LAB_N, FEAT, PIECE), F32),
            pltpu.VMEM((4, 4, HALF, PIECE), F32),
            pltpu.VMEM((4, 4, HALF, PIECE), F32),
            pltpu.VMEM((3, HALF, PIECE), F32),
            pltpu.VMEM((3, HALF, PIECE), F32),
            pltpu.VMEM((3, HALF, PIECE), F32),
            pltpu.VMEM((3, HALF, PIECE), F32),
            pltpu.VMEM((LAB_T, 128), F32),
            pltpu.VMEM((FLEET_T, 128), F32),
            pltpu.VMEM((FEAT, PIECE), F32),
            dma((4,)),
            dma((3,)),
            dma((ITERS, CHUNKS)),
            dma((ITERS,)),
            dma((4,)),
            dma((4,)),
            dma((2,)),
            dma((8,)),
            dma((3,)),
        ],
        name="sinkhorn",
        compiler_params=pltpu.CompilerParams(
            collective_id=0, has_side_effects=True, vmem_limit_bytes=56 * 2**20
        ),
    )(
        lab_features,
        fleet_features,
        lab_weight.reshape(LAB_T, 128),
        fleet_weight.reshape(FLEET_T, 128),
    )


def body(*args):
    *outs, flag = scaled(*args)

    def general():
        f, g, grad = log_domain(*args)
        return [f.reshape(LAB_T, 128), g.reshape(FLEET_T, 128), grad]

    f, g, grad = copy_outs(*lax.cond(flag[0] != 0, general, lambda: outs))
    return f.reshape(LAB), g.reshape(FLEET), grad


def solution(mesh):
    in_specs = (P(None, ("lab", "fleet")), P(None, ("fleet", "lab")), P("lab"), P("fleet"))
    out_specs = (P("lab"), P("fleet"), P(None, ("fleet", "lab")))
    return jax.shard_map(body, mesh=mesh, in_specs=in_specs, out_specs=out_specs, check_vma=False)
```

```python
import jax
import jax.numpy as jnp
from jax import lax
from jax.experimental import pallas as pl
from jax.experimental.pallas import tpu as pltpu
from jax.sharding import PartitionSpec as P


ITERS = 3
EPS = 0.5
LOG2E = 1.4426950408889634
LOW, HIGH = 2.0**-30, 2.0**60
LOW_RATIO, HIGH_RATIO = 2.0**-20, 2.0**20
MESH = pl.DeviceIdType.MESH
F32, BF16 = jnp.float32, jnp.bfloat16


def block_width():
    return 512


def split_columns(array, width):
    return array.reshape(array.shape[0], array.shape[1] // width, width).transpose(1, 0, 2)


def pair_cost(lab_part, sq_lab_part, fleet_part, sq_fleet_part):
    cross = lax.dot_general(
        lab_part, fleet_part, (((0,), (0,)), ((), ())), preferred_element_type=jnp.float32
    )
    return sq_lab_part[:, None] + sq_fleet_part[None, :] - 2.0 * cross


def square_sums(features):
    values = features.astype(jnp.float32)
    return jnp.sum(values * values, axis=0)


def ring(value, axis, visit, carry):
    n = lax.axis_size(axis)
    me = lax.axis_index(axis)

    right = [(i, (i + 1) % n) for i in range(n)]

    def step(k, state):
        block, carry = state
        carry = visit(lax.rem(me + n - k, n), block, carry)
        return lax.ppermute(block, axis, right), carry

    carry = visit(me, value, carry)
    return lax.fori_loop(1, n, step, (lax.ppermute(value, axis, right), carry))[1]


def gather(value, axis):
    def visit(index, block, out):
        return lax.dynamic_update_index_in_dim(out, block, index, 0)

    return ring(value, axis, visit, jnp.zeros((lax.axis_size(axis),) + value.shape, value.dtype))


def gather_columns(value, axis):
    return gather(value, axis).transpose(1, 0, 2).reshape(value.shape[0], -1)


def reduce_over(axis, top, total):
    tops, totals = gather(top, axis), gather(total, axis)
    top = jnp.max(tops, axis=0)
    total = jnp.sum(totals * jnp.exp(tops - top[None, :]), axis=0)
    return -EPS * (top + jnp.log(total))


def sum_own_columns(terms, axis):
    width = terms.shape[1] // lax.axis_size(axis)
    start = lax.axis_index(axis) * width

    def visit(index, block, out):
        return out + lax.dynamic_slice_in_dim(block, start, width, 1)

    return ring(terms, axis, visit, jnp.zeros((terms.shape[0], width), terms.dtype))


def log_domain(lab_features, fleet_features, lab_weight, fleet_weight):
    lab_block = gather_columns(lab_features, "fleet")
    fleet_block = gather_columns(fleet_features, "lab")
    sq_lab = square_sums(lab_block)
    sq_fleet = square_sums(fleet_block)
    log_a = jnp.log(lab_weight)
    log_b = jnp.log(fleet_weight)
    lab_count = lab_block.shape[1]
    fleet_count = fleet_block.shape[1]
    lab_width = block_width()
    fleet_width = block_width()
    lab_blocks = split_columns(lab_block, lab_width)
    fleet_blocks = split_columns(fleet_block, fleet_width)
    sq_lab_blocks = sq_lab.reshape(-1, lab_width)
    sq_fleet_blocks = sq_fleet.reshape(-1, fleet_width)
    log_b_blocks = log_b.reshape(-1, fleet_width)

    def lab_partial(fleet_pot):

        def lab_one_block(items):
            lab_part, sq_part = items
            score = (
                fleet_pot[None, :] - pair_cost(lab_part, sq_part, fleet_block, sq_fleet)
            ) / EPS + log_b[None, :]
            top = jnp.max(score, axis=1)
            return (top, jnp.sum(jnp.exp(score - top[:, None]), axis=1))

        top, total = lax.map(lab_one_block, (lab_blocks, sq_lab_blocks))
        return (top.reshape(lab_count), total.reshape(lab_count))

    def fleet_partial(lab_pot):

        def fleet_one_block(items):
            fleet_part, sq_part = items
            score = (
                lab_pot[:, None] - pair_cost(lab_block, sq_lab, fleet_part, sq_part)
            ) / EPS + log_a[:, None]
            top = jnp.max(score, axis=0)
            return (top, jnp.sum(jnp.exp(score - top[None, :]), axis=0))

        top, total = lax.map(fleet_one_block, (fleet_blocks, sq_fleet_blocks))
        return (top.reshape(fleet_count), total.reshape(fleet_count))

    def iteration(step, pots):
        lab_top, lab_total = lab_partial(pots[1])
        lab_pot = reduce_over("fleet", lab_top, lab_total)
        fleet_top, fleet_total = fleet_partial(lab_pot)
        return (lab_pot, reduce_over("lab", fleet_top, fleet_total))

    lab_pot, fleet_pot = lax.fori_loop(
        0, ITERS, iteration, (jnp.zeros((lab_count,), F32), jnp.zeros((fleet_count,), F32))
    )
    pot_blocks = fleet_pot.reshape(-1, fleet_width)
    lab_float = lab_block.astype(jnp.float32)

    def gradient_block(items):
        fleet_part, sq_part, pot_part, log_part = items
        cost = pair_cost(lab_block, sq_lab, fleet_part, sq_part)
        plan = jnp.exp(
            (lab_pot[:, None] + pot_part[None, :] - cost) / EPS + log_a[:, None] + log_part[None, :]
        )
        mass = jnp.sum(plan, axis=0)
        weighted = jnp.dot(
            lab_float, plan, preferred_element_type=jnp.float32, precision=lax.Precision.HIGHEST
        )
        return 2.0 * (fleet_part.astype(jnp.float32) * mass[None, :] - weighted)

    pieces = lax.map(gradient_block, (fleet_blocks, sq_fleet_blocks, pot_blocks, log_b_blocks))
    terms = pieces.transpose(1, 0, 2).reshape(fleet_block.shape[0], fleet_count)
    fleet_gradient = sum_own_columns(terms, "lab")
    return (lab_pot, fleet_pot, fleet_gradient)


FEAT = 64
PIECE = 256
LAB_N, FLEET_N = 16, 8
LAB, FLEET = PIECE * FLEET_N, PIECE * LAB_N
LAB_T, FLEET_T = LAB // 128, FLEET // 128
CHUNKS = 4
EXP_ROWS = 1024
HALF = FEAT // 2
ROWS = LAB // CHUNKS
CHUNK_T = LAB_T // CHUNKS
WAVE = FLEET_N // 2


def hops(offset):
    return sum(min(d, 4 - d) for d in offset)


LAB_OFFSETS = sorted(((z, x) for z in range(4) for x in range(4) if (z, x) != (0, 0)), key=hops)
LAB_OWN = LAB_N - 1
FLEET_OFFSETS = (4, 2, 6, 1, 3, 5, 7)
Y_OFFSETS = (2, 1, 3)
NEAR, MIDDLE, FAR = (LAB_OWN, 0, 1, 2, 3), (4, 5, 6, 7, 8, 9), (10, 11, 12, 13, 14)
GROUPS = (
    ((2, 2), (2, 1)),
    ((2, 3), (1, 2), (3, 2)),
    ((1, 1), (1, 3), (3, 1), (3, 3)),
    ((0, 2), (2, 0), (0, 1), (1, 0)),
    ((0, 3), (3, 0), (0, 0)),
)
DEPTH = 256


def owner_rows(position):
    piece = (position % WAVE) * 2 + position // WAVE
    return slice(2 * piece, 2 * piece + 2)


def dot(left, right):
    return lax.dot_general(left, right, (((1,), (0,)), ((), ())), preferred_element_type=F32)


def aligned(start, size, multiple):
    return pl.ds(pl.multiple_of(start, multiple), size)


def kernel(
    x_in, y_in, a_in, b_in, f_out, g_out, grad_out, flag_ref,
    a_ref, b_ref,
    xg, yg, xt, e_ref, lanes, spread, coef, sq_x, sq_y, scale, a_own, total_f, f_send, f_recv, g_send, g_recv,
    gx, gz, gx_sum, gz_sum, gxz, gzx, w_send, wx, wz, wx_sum, wz_sum, wxz, wzx, f_ref, g_ref, grad_ref,
    x_rs, y_rs, f_rs, g_rs, t_rs, wx_rs, wz_rs, w_rs, sent, in_s, out_s,
):
    me_l, me_f = lax.axis_index("lab"), lax.axis_index("fleet")
    core, chip = lax.rem(me_f, 2), me_f // 2
    me_z, me_x = me_l // 4, lax.rem(me_l, 4)

    def lab_at(dz, dx):
        return lax.rem(me_z + dz, 4) * 4 + lax.rem(me_x + dx, 4)

    fleet_to = [lax.rem(me_f + d, FLEET_N) for d in FLEET_OFFSETS]
    lab_to = [lab_at(dz, dx) for dz, dx in LAB_OFFSETS] + [me_l]
    lab_from = [lab_at(4 - dz, 4 - dx) for dz, dx in LAB_OFFSETS] + [me_l]

    barrier = pltpu.get_barrier_semaphore()
    for p in reversed(lab_to[:LAB_OWN]):
        pl.semaphore_signal(barrier, inc=1, device_id=(p, me_f), device_id_type=MESH)
    for p in fleet_to:
        pl.semaphore_signal(barrier, inc=1, device_id=(me_l, p), device_id_type=MESH)
    mine = core * WAVE + chip
    pairs = ((x_in, xg.at[mine]), (y_in, yg.at[LAB_OWN]), (a_in, a_ref), (b_in, b_ref))
    loads = [pltpu.make_async_copy(src, dst, in_s.at[i]) for i, (src, dst) in enumerate(pairs)]
    for c in loads:
        c.start()
    for c in loads:
        c.wait()
    with jax.named_scope("barrier"):
        pl.semaphore_wait(barrier, LAB_N - 1 + FLEET_N - 1)

    def copy_to_lab(n, src, dst, send, recv):
        return pltpu.make_async_remote_copy(
            src_ref=src, dst_ref=dst, send_sem=send, recv_sem=recv,
            device_id=(lab_to[n], me_f), device_id_type=MESH,
        )

    def copy_to_offset(dz, dx, src, dst, send, recv):
        return pltpu.make_async_remote_copy(
            src_ref=src, dst_ref=dst, send_sem=sent.at[send], recv_sem=recv,
            device_id=(lab_at(dz, dx), me_f), device_id_type=MESH,
        )

    def copy_to_fleet(to, src, dst, send, recv):
        return pltpu.make_async_remote_copy(
            src_ref=src, dst_ref=dst, send_sem=send, recv_sem=recv,
            device_id=(me_l, to), device_id_type=MESH,
        )

    def wait_sent(slots, send):
        copy_to_lab(0, slots, slots, sent.at[send], sent.at[send]).wait_send()

    def wait_received(slots, recv):
        copy_to_lab(0, slots, slots, sent.at[0], recv).wait_recv()

    sibling = chip * 2 + 1 - core
    x_copies = [
        copy_to_fleet(lax.rem(chip + d, 4) * 2 + core, xg.at[mine], xg.at[mine], sent.at[0], x_rs.at[n])
        for n, d in enumerate(Y_OFFSETS)
    ]
    x_copies.append(copy_to_fleet(sibling, xg.at[mine], xg.at[mine], sent.at[0], x_rs.at[3]))
    y_copies = [
        copy_to_lab(n, yg.at[LAB_OWN], yg.at[n], sent.at[1], y_rs.at[0 if n in NEAR else 1 if n in MIDDLE else 2]) for n in range(LAB_N - 1)
    ]
    for c in x_copies + y_copies:
        c.start()
    for at in range(FLEET_N):
        q, i = divmod(2 * at, CHUNK_T)
        a_own[q, i : i + 2, :] = a_ref[owner_rows(at), :]

    def x_prep(at):
        x = xg[at].astype(F32)
        xt[aligned(at * PIECE, PIECE, PIECE), :] = x.T.astype(BF16)
        sq = jnp.sum(x * x, axis=0, keepdims=True)
        for h in range(2):
            sq_x[pl.ds(2 * at + h, 1), :] = sq[:, h * 128 : (h + 1) * 128]

    def y_prep(n):
        y = yg[n].astype(F32)
        sq = jnp.sum(y * y, axis=0, keepdims=True)
        for h in range(2):
            row = pl.ds(2 * lab_from[n] + h, 1)
            part = sq[:, h * 128 : (h + 1) * 128]
            sq_y[row, :] = part
            scale[row, :] = b_ref[row, :] * jnp.exp2(part * (-LOG2E / EPS))

    def exp_rows(start, size, slots, first):
        rows = aligned(start, size, size)
        left = xt[rows, :]
        total = None if first else lanes[rows, :]
        for n in slots:
            part = jnp.exp2(dot(left, yg[n]) * (2.0 * LOG2E / EPS))
            e_ref[rows, aligned(lab_from[n] * PIECE, PIECE, PIECE)] = part
            for h in range(2):
                term = part[:, h * 128 : (h + 1) * 128] * scale[pl.ds(2 * lab_from[n] + h, 1), :]
                total = term if total is None else total + term
        lanes[rows, :] = total

    def copy_sums(k, q, n):
        return copy_to_fleet(fleet_to[n], f_send.at[k, q], f_recv.at[k, me_f, q], sent.at[2], f_rs.at[k, q])

    def send_sums(k, q):
        for t in range(CHUNK_T):
            rows = aligned(q * ROWS + t * 128, 128, 128)
            f_send[k, q, t : t + 1, :] = jnp.sum(lanes[rows, :].T, axis=0, keepdims=True)
        for n in range(FLEET_N - 1):
            copy_sums(k, q, n).start()
        f_recv[k, me_f, q] = f_send[k, q]

    y_prep(LAB_OWN)
    x_prep(mine)
    with jax.named_scope("x_wait"):
        for n, d in enumerate(Y_OFFSETS):
            x_copies[n].wait_recv()
            at = core * WAVE + lax.rem(chip + 4 - d, 4)
            copy_to_fleet(sibling, xg.at[at], xg.at[at], sent.at[0], x_rs.at[3]).start()
        for d in Y_OFFSETS:
            x_prep(core * WAVE + lax.rem(chip + 4 - d, 4))
    with jax.named_scope("y_near"):
        wait_received(yg.at[0 : len(NEAR) - 1], y_rs.at[0])
        for n in NEAR[1:]:
            y_prep(n)
    with jax.named_scope("exp_first"):
        exp_rows(core * EXP_ROWS, EXP_ROWS, NEAR, True)
    with jax.named_scope("x_sibling"):
        wait_received(xg.at[0:WAVE], x_rs.at[3])
        for i in range(WAVE):
            x_prep((1 - core) * WAVE + i)
    with jax.named_scope("exp_second"):
        exp_rows((1 - core) * EXP_ROWS, EXP_ROWS, NEAR, True)
    with jax.named_scope("y_middle"):
        wait_received(yg.at[0 : len(MIDDLE)], y_rs.at[1])
        for n in MIDDLE:
            y_prep(n)

    def exp_middle(i, carry):
        exp_rows(i * EXP_ROWS, EXP_ROWS, MIDDLE, False)
        return carry

    with jax.named_scope("exp_middle"):
        lax.fori_loop(0, LAB // EXP_ROWS, exp_middle, 0)
    with jax.named_scope("y_far"):
        wait_received(yg.at[0 : len(FAR)], y_rs.at[2])
        for n in FAR:
            y_prep(n)

    def exp_far(q, carry):
        exp_rows(q * ROWS, ROWS, FAR, False)
        send_sums(0, q)
        return carry

    with jax.named_scope("exp_far"):
        lax.fori_loop(0, CHUNKS, exp_far, 0)

    def lab_pass(k):
        beta = [jnp.broadcast_to(scale[t : t + 1, :], (8, 128)) for t in range(FLEET_T)]

        def rows_of(r, carry):
            for i in range(8):
                rows = aligned(r * 64 + 8 * i, 8, 8)
                acc = [e_ref[rows, t * 128 : (t + 1) * 128] * beta[t] for t in range(4)]
                for t in range(4, FLEET_T):
                    acc[t % 4] = acc[t % 4] + e_ref[rows, t * 128 : (t + 1) * 128] * beta[t]
                lanes[rows, :] = (acc[0] + acc[1]) + (acc[2] + acc[3])
            return carry

        def chunk(q, carry):
            lax.fori_loop(q * (ROWS // 64), (q + 1) * (ROWS // 64), rows_of, 0)
            send_sums(k, q)
            return carry

        with jax.named_scope("lab_pass"):
            lax.fori_loop(0, CHUNKS, chunk, 0)

    def alpha_of(k, q):
        with jax.named_scope("lab_sums"):
            wait_received(f_recv.at[k, 0 : FLEET_N - 1, q], f_rs.at[k, q])
        total = f_recv[k, 0, q]
        for p in range(1, FLEET_N):
            total = total + f_recv[k, p, q]
        good = (total > LOW) & (total < HIGH)
        if k > 0:
            before = total_f[q]
            good = good & (total > before * LOW_RATIO) & (total < before * HIGH_RATIO)
        total = jnp.where(good, total, jnp.nan)
        total_f[q] = total
        return a_own[q] / total

    def last_alpha(q, alpha):
        potential = sq_x[q * CHUNK_T : (q + 1) * CHUNK_T, :] - EPS * jnp.log(total_f[q])
        for i in range(CHUNK_T // 2):
            f_ref[owner_rows(q * CHUNK_T // 2 + i), :] = potential[2 * i : 2 * i + 2]
        for t in range(CHUNK_T):
            at = q * CHUNK_T + t
            cols = slice(at * 128, (at + 1) * 128)
            x = xg[at // 2, :, (at % 2) * 128 : (at % 2 + 1) * 128].astype(F32) * alpha[t : t + 1, :]
            high = x.astype(BF16)
            coef[0:FEAT, cols] = high
            coef[FEAT : 2 * FEAT, cols] = (x - high.astype(F32)).astype(BF16)

    def fleet_pass(k):
        acc = tuple(jnp.zeros((8, 128), F32) for _ in range(FLEET_T))
        for q in range(CHUNKS):
            alpha = alpha_of(k, q)
            if k == ITERS - 1:
                last_alpha(q, alpha)
            with jax.named_scope("fleet_pass"):
                for t in range(CHUNK_T):
                    rows = slice(q * ROWS + t * 128, q * ROWS + (t + 1) * 128)
                    spread[rows, :] = jnp.broadcast_to(alpha[t : t + 1, :], (128, 128)).T

                def rows_of(r, acc):
                    rows = aligned(r * 8, 8, 8)
                    factor = spread[rows, :]
                    return tuple(acc[t] + e_ref[rows, t * 128 : (t + 1) * 128] * factor for t in range(FLEET_T))

                acc = lax.fori_loop(q * (ROWS // 8), (q + 1) * (ROWS // 8), rows_of, acc, unroll=8)
        for t in range(FLEET_T):
            g_send[k, t : t + 1, :] = jnp.sum(acc[t], axis=0, keepdims=True)

    def start_fleet_sums(k):
        for n in reversed(range(LAB_N - 1)):
            copy_to_lab(n, g_send.at[k], g_recv.at[k, me_l], sent.at[3], g_rs.at[k]).start()
        g_recv[k, me_l] = g_send[k]

    def end_fleet_sums(k):
        with jax.named_scope("fleet_sums"):
            wait_received(g_recv.at[k, 0 : LAB_N - 1], g_rs.at[k])
        total = g_recv[k, 0]
        for p in range(1, LAB_N):
            total = total + g_recv[k, p]
        return total

    for k in range(ITERS - 1):
        fleet_pass(k)
        start_fleet_sums(k)
        total = end_fleet_sums(k)
        total = jnp.where((total > LOW) & (total < HIGH), total, jnp.nan)
        scale[...] = b_ref[...] / total
        lab_pass(k + 1)

    fleet_pass(ITERS - 1)
    mid = FLEET_T // 2
    for d in (2, 1, 3):
        copy_to_offset(0, d, g_send.at[ITERS - 1, 0:mid], gx.at[me_x], 8, t_rs.at[0]).start()
        copy_to_offset(d, 0, g_send.at[ITERS - 1, mid:FLEET_T], gz.at[me_z], 9, t_rs.at[1]).start()
    gx[me_x] = g_send[ITERS - 1, 0:mid]
    gz[me_z] = g_send[ITERS - 1, mid:FLEET_T]

    def forward_totals():
        with jax.named_scope("totals_first"):
            wait_received(gx.at[0:3], t_rs.at[0])
            wait_received(gz.at[0:3], t_rs.at[1])
        gx_sum[...] = sum_of([gx[i] for i in range(4)])
        gz_sum[...] = sum_of([gz[i] for i in range(4)])
        for d in (2, 1, 3):
            copy_to_offset(d, 0, gx_sum, gxz.at[me_z], 10, t_rs.at[2]).start()
            copy_to_offset(0, d, gz_sum, gzx.at[me_x], 11, t_rs.at[3]).start()
        gxz[me_z] = gx_sum[...]
        gzx[me_x] = gz_sum[...]

    outs = [pltpu.make_async_copy(src, dst, out_s.at[i]) for i, (src, dst) in enumerate(
        ((f_ref, f_out), (g_ref, g_out), (grad_ref, grad_out)))]
    outs[0].start()

    def sum_of(parts):
        return (parts[0] + parts[1]) + (parts[2] + parts[3])

    def forward(offsets):
        with jax.named_scope("weighted_first"):
            for d in offsets:
                wait_received(wx.at[0:3, d], wx_rs.at[d])
                wx_sum[d - 1] = sum_of([wx[i, d] for i in range(4)])
                copy_to_offset(d, 0, wx_sum.at[d - 1], wxz.at[d - 1], 6, w_rs.at[0]).start()
                wait_received(wz.at[0:3, d], wz_rs.at[d])
                wz_sum[d - 1] = sum_of([wz[i, d] for i in range(4)])
                copy_to_offset(0, d, wz_sum.at[d - 1], wzx.at[d - 1], 7, w_rs.at[1]).start()

    for number, group in enumerate(GROUPS):
        with jax.named_scope("weighted"):
            for dz, dx in group:
                at = dz * 4 + dx
                cols = aligned(lab_at(dz, dx) * PIECE, PIECE, PIECE)
                part = None
                for k in range(LAB // DEPTH):
                    rows = slice(k * DEPTH, (k + 1) * DEPTH)
                    e, left = e_ref[rows, cols], coef[:, rows]
                    high = e.astype(BF16)
                    term = dot(left, high) + dot(left, (e - high.astype(F32)).astype(BF16))
                    part = term if part is None else part + term
                weighted = part[:FEAT] + part[FEAT:]
                if dx == 0:
                    wx[3, dz] = weighted[:HALF]
                if dz == 0:
                    wz[3, dx] = weighted[HALF:]
                w_send[at] = weighted
            for dz, dx in group:
                at = dz * 4 + dx
                if dx != 0:
                    copy_to_offset(0, dx, w_send.at[at, 0:HALF], wx.at[dx - 1, dz], 4, wx_rs.at[dz]).start()
                if dz != 0:
                    copy_to_offset(dz, 0, w_send.at[at, HALF:FEAT], wz.at[dz - 1, dx], 5, wz_rs.at[dx]).start()

        if number == 2:
            forward_totals()
    forward((2, 1, 3))
    with jax.named_scope("totals_second"):
        wait_received(gxz.at[0:3], t_rs.at[2])
        wait_received(gzx.at[0:3], t_rs.at[3])
    scale[0:mid, :] = sum_of([gxz[i] for i in range(4)])
    scale[mid:FLEET_T, :] = sum_of([gzx[i] for i in range(4)])
    total = scale[...]
    flag_ref[0] = jnp.where(jnp.sum(jnp.where(total == total, 0.0, 1.0)) > 0.0, 1, 0)
    g_ref[...] = sq_y[...] - EPS * jnp.log(total)
    outs[1].start()
    with jax.named_scope("weighted_own"):
        wait_received(wx.at[0:3, 0], wx_rs.at[0])
        wait_received(wz.at[0:3, 0], wz_rs.at[0])
    upper = sum_of([wx[i, 0] for i in range(4)])
    lower = sum_of([wz[i, 0] for i in range(4)])
    with jax.named_scope("weighted_second"):
        wait_received(wxz.at[0:3], w_rs.at[0])
        wait_received(wzx.at[0:3], w_rs.at[1])
    upper = sum_of([upper] + [wxz[i] for i in range(3)])
    lower = sum_of([lower] + [wzx[i] for i in range(3)])
    for h in range(2):
        cols = slice(h * 128, (h + 1) * 128)
        row = pl.ds(2 * me_l + h, 1)
        factor, inverse = 2.0 * b_ref[row, :], 1.0 / scale[row, :]
        for part, rows in ((upper, slice(0, HALF)), (lower, slice(HALF, FEAT))):
            grad_ref[rows, cols] = factor * (yg[LAB_OWN, rows, cols].astype(F32) - part[:, cols] * inverse)
    outs[2].start()
    with jax.named_scope("outputs"):
        wait_sent(xg.at[0 : FLEET_N - 1], 0)
        wait_sent(yg.at[0 : LAB_N - 1], 1)
        wait_sent(f_recv.at[:, 0 : FLEET_N - 1], 2)
        wait_sent(g_recv.at[:, 0 : LAB_N - 1], 3)
        for i, slots in enumerate((wx, wz, wxz, wzx, gx, gz, gxz, gzx)):
            wait_sent(slots.at[0:3], 4 + i)
        for c in outs:
            c.wait()


OUT_SHAPES = [
    jax.ShapeDtypeStruct((LAB_T, 128), F32),
    jax.ShapeDtypeStruct((FLEET_T, 128), F32),
    jax.ShapeDtypeStruct((FEAT, PIECE), F32),
]


def copy_kernel(*refs):
    for i in range(3):
        refs[3 + i][...] = refs[i][...]


def copy_outs(*outs):
    vmem = pl.BlockSpec(memory_space=pltpu.VMEM)
    return pl.pallas_call(
        copy_kernel, out_shape=OUT_SHAPES, in_specs=[vmem] * 3, out_specs=[vmem] * 3, name="outputs"
    )(*outs)


def scaled(lab_features, fleet_features, lab_weight, fleet_weight):
    anywhere = pl.BlockSpec(memory_space=pl.ANY)
    dma = pltpu.SemaphoreType.DMA
    return pl.pallas_call(
        kernel,
        out_shape=OUT_SHAPES + [jax.ShapeDtypeStruct((1,), jnp.int32)],
        in_specs=[anywhere] * 4,
        out_specs=[anywhere] * 3 + [pl.BlockSpec(memory_space=pltpu.SMEM)],
        scratch_shapes=[
            pltpu.VMEM((LAB_T, 128), F32),
            pltpu.VMEM((FLEET_T, 128), F32),
            pltpu.VMEM((FLEET_N, FEAT, PIECE), BF16),
            pltpu.VMEM((LAB_N, FEAT, PIECE), BF16),
            pltpu.VMEM((LAB, FEAT), BF16),
            pltpu.VMEM((LAB, FLEET), F32),
            pltpu.VMEM((LAB, 128), F32),
            pltpu.VMEM((LAB, 128), F32),
            pltpu.VMEM((2 * FEAT, LAB), BF16),
            pltpu.VMEM((LAB_T, 128), F32),
            pltpu.VMEM((FLEET_T, 128), F32),
            pltpu.VMEM((FLEET_T, 128), F32),
            pltpu.VMEM((CHUNKS, CHUNK_T, 128), F32),
            pltpu.VMEM((CHUNKS, CHUNK_T, 128), F32),
            pltpu.VMEM((ITERS, CHUNKS, CHUNK_T, 128), F32),
            pltpu.VMEM((ITERS, FLEET_N, CHUNKS, CHUNK_T, 128), F32),
            pltpu.VMEM((ITERS, FLEET_T, 128), F32),
            pltpu.VMEM((ITERS - 1, LAB_N, FLEET_T, 128), F32),
            pltpu.VMEM((4, FLEET_T // 2, 128), F32),
            pltpu.VMEM((4, FLEET_T // 2, 128), F32),
            pltpu.VMEM((FLEET_T // 2, 128), F32),
            pltpu.VMEM((FLEET_T // 2, 128), F32),
            pltpu.VMEM((4, FLEET_T // 2, 128), F32),
            pltpu.VMEM((4, FLEET_T // 2, 128), F32),
            pltpu.VMEM((LAB_N, FEAT, PIECE), F32),
            pltpu.VMEM((4, 4, HALF, PIECE), F32),
            pltpu.VMEM((4, 4, HALF, PIECE), F32),
            pltpu.VMEM((3, HALF, PIECE), F32),
            pltpu.VMEM((3, HALF, PIECE), F32),
            pltpu.VMEM((3, HALF, PIECE), F32),
            pltpu.VMEM((3, HALF, PIECE), F32),
            pltpu.VMEM((LAB_T, 128), F32),
            pltpu.VMEM((FLEET_T, 128), F32),
            pltpu.VMEM((FEAT, PIECE), F32),
            dma((4,)),
            dma((3,)),
            dma((ITERS, CHUNKS)),
            dma((ITERS - 1,)),
            dma((4,)),
            dma((4,)),
            dma((4,)),
            dma((2,)),
            dma((12,)),
            dma((4,)),
            dma((3,)),
        ],
        name="sinkhorn",
        compiler_params=pltpu.CompilerParams(
            collective_id=0, has_side_effects=True, vmem_limit_bytes=56 * 2**20
        ),
    )(
        lab_features,
        fleet_features,
        lab_weight.reshape(LAB_T, 128),
        fleet_weight.reshape(FLEET_T, 128),
    )


def body(*args):
    *outs, flag = scaled(*args)

    def general():
        f, g, grad = log_domain(*args)
        return [f.reshape(LAB_T, 128), g.reshape(FLEET_T, 128), grad]

    f, g, grad = copy_outs(*lax.cond(flag[0] != 0, general, lambda: outs))
    return f.reshape(LAB), g.reshape(FLEET), grad


def solution(mesh):
    in_specs = (P(None, ("lab", "fleet")), P(None, ("fleet", "lab")), P("lab"), P("fleet"))
    out_specs = (P("lab"), P("fleet"), P(None, ("fleet", "lab")))
    return jax.shard_map(body, mesh=mesh, in_specs=in_specs, out_specs=out_specs, check_vma=False)
```

```python
import jax
import jax.numpy as jnp
from jax import lax
from jax.experimental import pallas as pl
from jax.experimental.pallas import tpu as pltpu
from jax.sharding import PartitionSpec as P


ITERS = 3
EPS = 0.5
LOG2E = 1.4426950408889634
LOW, HIGH = 2.0**-30, 2.0**60
LOW_RATIO, HIGH_RATIO = 2.0**-20, 2.0**20
MESH = pl.DeviceIdType.MESH
F32, BF16 = jnp.float32, jnp.bfloat16


def block_width():
    return 512


def split_columns(array, width):
    return array.reshape(array.shape[0], array.shape[1] // width, width).transpose(1, 0, 2)


def pair_cost(lab_part, sq_lab_part, fleet_part, sq_fleet_part):
    cross = lax.dot_general(
        lab_part, fleet_part, (((0,), (0,)), ((), ())), preferred_element_type=jnp.float32
    )
    return sq_lab_part[:, None] + sq_fleet_part[None, :] - 2.0 * cross


def square_sums(features):
    values = features.astype(jnp.float32)
    return jnp.sum(values * values, axis=0)


def ring(value, axis, visit, carry):
    n = lax.axis_size(axis)
    me = lax.axis_index(axis)

    right = [(i, (i + 1) % n) for i in range(n)]

    def step(k, state):
        block, carry = state
        carry = visit(lax.rem(me + n - k, n), block, carry)
        return lax.ppermute(block, axis, right), carry

    carry = visit(me, value, carry)
    return lax.fori_loop(1, n, step, (lax.ppermute(value, axis, right), carry))[1]


def gather(value, axis):
    def visit(index, block, out):
        return lax.dynamic_update_index_in_dim(out, block, index, 0)

    return ring(value, axis, visit, jnp.zeros((lax.axis_size(axis),) + value.shape, value.dtype))


def gather_columns(value, axis):
    return gather(value, axis).transpose(1, 0, 2).reshape(value.shape[0], -1)


def reduce_over(axis, top, total):
    tops, totals = gather(top, axis), gather(total, axis)
    top = jnp.max(tops, axis=0)
    total = jnp.sum(totals * jnp.exp(tops - top[None, :]), axis=0)
    return -EPS * (top + jnp.log(total))


def sum_own_columns(terms, axis):
    width = terms.shape[1] // lax.axis_size(axis)
    start = lax.axis_index(axis) * width

    def visit(index, block, out):
        return out + lax.dynamic_slice_in_dim(block, start, width, 1)

    return ring(terms, axis, visit, jnp.zeros((terms.shape[0], width), terms.dtype))


def log_domain(lab_features, fleet_features, lab_weight, fleet_weight):
    lab_block = gather_columns(lab_features, "fleet")
    fleet_block = gather_columns(fleet_features, "lab")
    sq_lab = square_sums(lab_block)
    sq_fleet = square_sums(fleet_block)
    log_a = jnp.log(lab_weight)
    log_b = jnp.log(fleet_weight)
    lab_count = lab_block.shape[1]
    fleet_count = fleet_block.shape[1]
    lab_width = block_width()
    fleet_width = block_width()
    lab_blocks = split_columns(lab_block, lab_width)
    fleet_blocks = split_columns(fleet_block, fleet_width)
    sq_lab_blocks = sq_lab.reshape(-1, lab_width)
    sq_fleet_blocks = sq_fleet.reshape(-1, fleet_width)
    log_b_blocks = log_b.reshape(-1, fleet_width)

    def lab_partial(fleet_pot):

        def lab_one_block(items):
            lab_part, sq_part = items
            score = (
                fleet_pot[None, :] - pair_cost(lab_part, sq_part, fleet_block, sq_fleet)
            ) / EPS + log_b[None, :]
            top = jnp.max(score, axis=1)
            return (top, jnp.sum(jnp.exp(score - top[:, None]), axis=1))

        top, total = lax.map(lab_one_block, (lab_blocks, sq_lab_blocks))
        return (top.reshape(lab_count), total.reshape(lab_count))

    def fleet_partial(lab_pot):

        def fleet_one_block(items):
            fleet_part, sq_part = items
            score = (
                lab_pot[:, None] - pair_cost(lab_block, sq_lab, fleet_part, sq_part)
            ) / EPS + log_a[:, None]
            top = jnp.max(score, axis=0)
            return (top, jnp.sum(jnp.exp(score - top[None, :]), axis=0))

        top, total = lax.map(fleet_one_block, (fleet_blocks, sq_fleet_blocks))
        return (top.reshape(fleet_count), total.reshape(fleet_count))

    def iteration(step, pots):
        lab_top, lab_total = lab_partial(pots[1])
        lab_pot = reduce_over("fleet", lab_top, lab_total)
        fleet_top, fleet_total = fleet_partial(lab_pot)
        return (lab_pot, reduce_over("lab", fleet_top, fleet_total))

    lab_pot, fleet_pot = lax.fori_loop(
        0, ITERS, iteration, (jnp.zeros((lab_count,), F32), jnp.zeros((fleet_count,), F32))
    )
    pot_blocks = fleet_pot.reshape(-1, fleet_width)
    lab_float = lab_block.astype(jnp.float32)

    def gradient_block(items):
        fleet_part, sq_part, pot_part, log_part = items
        cost = pair_cost(lab_block, sq_lab, fleet_part, sq_part)
        plan = jnp.exp(
            (lab_pot[:, None] + pot_part[None, :] - cost) / EPS + log_a[:, None] + log_part[None, :]
        )
        mass = jnp.sum(plan, axis=0)
        weighted = jnp.dot(
            lab_float, plan, preferred_element_type=jnp.float32, precision=lax.Precision.HIGHEST
        )
        return 2.0 * (fleet_part.astype(jnp.float32) * mass[None, :] - weighted)

    pieces = lax.map(gradient_block, (fleet_blocks, sq_fleet_blocks, pot_blocks, log_b_blocks))
    terms = pieces.transpose(1, 0, 2).reshape(fleet_block.shape[0], fleet_count)
    fleet_gradient = sum_own_columns(terms, "lab")
    return (lab_pot, fleet_pot, fleet_gradient)


FEAT = 64
PIECE = 256
LAB_N, FLEET_N = 16, 8
LAB, FLEET = PIECE * FLEET_N, PIECE * LAB_N
LAB_T, FLEET_T = LAB // 128, FLEET // 128
CHUNKS = 4
EXP_ROWS = 1024
HALF = FEAT // 2
ROWS = LAB // CHUNKS
CHUNK_T = LAB_T // CHUNKS
WAVE = FLEET_N // 2


def hops(offset):
    return sum(min(d, 4 - d) for d in offset)


LAB_OFFSETS = sorted(((z, x) for z in range(4) for x in range(4) if (z, x) != (0, 0)), key=hops)
LAB_OWN = LAB_N - 1
FLEET_OFFSETS = (4, 2, 6, 1, 3, 5, 7)
Y_OFFSETS = (2, 1, 3)
NEAR, MIDDLE, FAR = (LAB_OWN, 0, 1, 2, 3), (4, 5, 6, 7, 8, 9), (10, 11, 12, 13, 14)
GROUPS = (
    ((2, 2), (2, 1)),
    ((2, 3), (1, 2), (3, 2)),
    ((1, 1), (1, 3), (3, 1), (3, 3)),
    ((0, 2), (2, 0), (0, 1), (1, 0)),
    ((0, 3), (3, 0), (0, 0)),
)
DEPTH = 256


def slot_from(dz, dx):
    back = (-dz % 4, -dx % 4)
    return LAB_OWN if back == (0, 0) else LAB_OFFSETS.index(back)


def owner_rows(position):
    piece = (position % WAVE) * 2 + position // WAVE
    return slice(2 * piece, 2 * piece + 2)


def dot(left, right):
    return lax.dot_general(left, right, (((1,), (0,)), ((), ())), preferred_element_type=F32)


def aligned(start, size, multiple):
    return pl.ds(pl.multiple_of(start, multiple), size)


def kernel(
    x_in, y_in, a_in, b_in, f_ref, g_ref, grad_ref, flag_ref,
    a_ref, b_ref,
    xg, yg, xt, e_ref, lanes, spread, coef, sq_x, sq_y, scale, quotient, a_own, total_f, f_send, f_recv, g_send, g_recv,
    gx, gz, gx_sum, gz_sum, gxz, gzx, w_send, wx, wz, wx_sum, wz_sum, wxz, wzx,
    x_rs, y_rs, f_rs, g_rs, t_rs, wx_rs, wz_rs, w_rs, sent, in_s,
):
    me_l, me_f = lax.axis_index("lab"), lax.axis_index("fleet")
    core, chip = lax.rem(me_f, 2), me_f // 2
    me_z, me_x = me_l // 4, lax.rem(me_l, 4)

    def lab_at(dz, dx):
        return lax.rem(me_z + dz, 4) * 4 + lax.rem(me_x + dx, 4)

    fleet_to = [lax.rem(me_f + d, FLEET_N) for d in FLEET_OFFSETS]
    lab_to = [lab_at(dz, dx) for dz, dx in LAB_OFFSETS] + [me_l]
    lab_from = [lab_at(4 - dz, 4 - dx) for dz, dx in LAB_OFFSETS] + [me_l]

    barrier = pltpu.get_barrier_semaphore()
    for p in reversed(lab_to[:LAB_OWN]):
        pl.semaphore_signal(barrier, inc=1, device_id=(p, me_f), device_id_type=MESH)
    for p in fleet_to:
        pl.semaphore_signal(barrier, inc=1, device_id=(me_l, p), device_id_type=MESH)
    mine = core * WAVE + chip
    pairs = ((x_in, xg.at[mine]), (y_in, yg.at[LAB_OWN]), (a_in, a_ref), (b_in, b_ref))
    loads = [pltpu.make_async_copy(src, dst, in_s.at[i]) for i, (src, dst) in enumerate(pairs)]
    for c in loads:
        c.start()
    for c in loads:
        c.wait()
    with jax.named_scope("barrier"):
        pl.semaphore_wait(barrier, LAB_N - 1 + FLEET_N - 1)

    def copy_to_lab(n, src, dst, send, recv):
        return pltpu.make_async_remote_copy(
            src_ref=src, dst_ref=dst, send_sem=send, recv_sem=recv,
            device_id=(lab_to[n], me_f), device_id_type=MESH,
        )

    def copy_to_offset(dz, dx, src, dst, send, recv):
        return pltpu.make_async_remote_copy(
            src_ref=src, dst_ref=dst, send_sem=sent.at[send], recv_sem=recv,
            device_id=(lab_at(dz, dx), me_f), device_id_type=MESH,
        )

    def copy_to_fleet(to, src, dst, send, recv):
        return pltpu.make_async_remote_copy(
            src_ref=src, dst_ref=dst, send_sem=send, recv_sem=recv,
            device_id=(me_l, to), device_id_type=MESH,
        )

    def wait_sent(slots, send):
        copy_to_lab(0, slots, slots, sent.at[send], sent.at[send]).wait_send()

    def wait_received(slots, recv):
        copy_to_lab(0, slots, slots, sent.at[0], recv).wait_recv()

    sibling = chip * 2 + 1 - core
    x_copies = [
        copy_to_fleet(lax.rem(chip + d, 4) * 2 + core, xg.at[mine], xg.at[mine], sent.at[0], x_rs.at[n])
        for n, d in enumerate(Y_OFFSETS)
    ]
    x_copies.append(copy_to_fleet(sibling, xg.at[mine], xg.at[mine], sent.at[0], x_rs.at[3]))
    y_copies = [
        copy_to_lab(n, yg.at[LAB_OWN], yg.at[n], sent.at[1], y_rs.at[0 if n in NEAR else 1 if n in MIDDLE else 2]) for n in range(LAB_N - 1)
    ]
    for c in x_copies + y_copies:
        c.start()
    for at in range(FLEET_N):
        q, i = divmod(2 * at, CHUNK_T)
        a_own[q, i : i + 2, :] = a_ref[owner_rows(at), :]

    def fleet_row(t):
        return pl.ds(2 * lab_from[t // 2] + t % 2, 1)

    def x_prep(at):
        x = xg[at].astype(F32)
        xt[aligned(at * PIECE, PIECE, PIECE), :] = x.T.astype(BF16)
        sq = jnp.sum(x * x, axis=0, keepdims=True)
        for h in range(2):
            sq_x[pl.ds(2 * at + h, 1), :] = sq[:, h * 128 : (h + 1) * 128]

    def y_prep(n):
        y = yg[n].astype(F32)
        sq = jnp.sum(y * y, axis=0, keepdims=True)
        for h in range(2):
            row = fleet_row(2 * n + h)
            part = sq[:, h * 128 : (h + 1) * 128]
            sq_y[row, :] = part
            scale[2 * n + h : 2 * n + h + 1, :] = b_ref[row, :] * jnp.exp2(part * (-LOG2E / EPS))

    def exp_rows(start, size, slots, first):
        rows = aligned(start, size, size)
        left = xt[rows, :]
        total = None if first else lanes[rows, :]
        for n in slots:
            part = jnp.exp2(dot(left, yg[n]) * (2.0 * LOG2E / EPS))
            e_ref[rows, n * PIECE : (n + 1) * PIECE] = part
            for h in range(2):
                term = part[:, h * 128 : (h + 1) * 128] * scale[2 * n + h : 2 * n + h + 1, :]
                total = term if total is None else total + term
        lanes[rows, :] = total

    def copy_sums(k, q, n):
        return copy_to_fleet(fleet_to[n], f_send.at[k, q], f_recv.at[k, me_f, q], sent.at[2], f_rs.at[k, q])

    def send_sums(k, q):
        for t in range(CHUNK_T):
            rows = aligned(q * ROWS + t * 128, 128, 128)
            f_send[k, q, t : t + 1, :] = jnp.sum(lanes[rows, :].T, axis=0, keepdims=True)
        for n in range(FLEET_N - 1):
            copy_sums(k, q, n).start()
        f_recv[k, me_f, q] = f_send[k, q]

    y_prep(LAB_OWN)
    x_prep(mine)
    with jax.named_scope("x_wait"):
        for n, d in enumerate(Y_OFFSETS):
            x_copies[n].wait_recv()
            at = core * WAVE + lax.rem(chip + 4 - d, 4)
            copy_to_fleet(sibling, xg.at[at], xg.at[at], sent.at[0], x_rs.at[3]).start()
        for d in Y_OFFSETS:
            x_prep(core * WAVE + lax.rem(chip + 4 - d, 4))
    with jax.named_scope("y_near"):
        wait_received(yg.at[0 : len(NEAR) - 1], y_rs.at[0])
        for n in NEAR[1:]:
            y_prep(n)
    with jax.named_scope("exp_first"):
        exp_rows(core * EXP_ROWS, EXP_ROWS, NEAR, True)
    with jax.named_scope("x_sibling"):
        wait_received(xg.at[0:WAVE], x_rs.at[3])
        for i in range(WAVE):
            x_prep((1 - core) * WAVE + i)
    with jax.named_scope("exp_second"):
        exp_rows((1 - core) * EXP_ROWS, EXP_ROWS, NEAR, True)
    with jax.named_scope("y_middle"):
        wait_received(yg.at[0 : len(MIDDLE)], y_rs.at[1])
        for n in MIDDLE:
            y_prep(n)

    def exp_middle(i, carry):
        exp_rows(i * EXP_ROWS, EXP_ROWS, MIDDLE, False)
        return carry

    with jax.named_scope("exp_middle"):
        lax.fori_loop(0, LAB // EXP_ROWS, exp_middle, 0)
    with jax.named_scope("y_far"):
        wait_received(yg.at[0 : len(FAR)], y_rs.at[2])
        for n in FAR:
            y_prep(n)

    def exp_far(q, carry):
        exp_rows(q * ROWS, ROWS, FAR, False)
        send_sums(0, q)
        return carry

    with jax.named_scope("exp_far"):
        lax.fori_loop(0, CHUNKS, exp_far, 0)

    def lab_pass(k):
        beta = [jnp.broadcast_to(scale[t : t + 1, :], (8, 128)) for t in range(FLEET_T)]

        def rows_of(r, carry):
            for i in range(8):
                rows = aligned(r * 64 + 8 * i, 8, 8)
                acc = [e_ref[rows, t * 128 : (t + 1) * 128] * beta[t] for t in range(4)]
                for t in range(4, FLEET_T):
                    acc[t % 4] = acc[t % 4] + e_ref[rows, t * 128 : (t + 1) * 128] * beta[t]
                lanes[rows, :] = (acc[0] + acc[1]) + (acc[2] + acc[3])
            return carry

        def chunk(q, carry):
            lax.fori_loop(q * (ROWS // 64), (q + 1) * (ROWS // 64), rows_of, 0)
            send_sums(k, q)
            return carry

        with jax.named_scope("lab_pass"):
            lax.fori_loop(0, CHUNKS, chunk, 0)

    def alpha_of(k, q):
        with jax.named_scope("lab_sums"):
            wait_received(f_recv.at[k, 0 : FLEET_N - 1, q], f_rs.at[k, q])
        total = f_recv[k, 0, q]
        for p in range(1, FLEET_N):
            total = total + f_recv[k, p, q]
        good = (total > LOW) & (total < HIGH)
        if k > 0:
            before = total_f[q]
            good = good & (total > before * LOW_RATIO) & (total < before * HIGH_RATIO)
        total = jnp.where(good, total, jnp.nan)
        total_f[q] = total
        return a_own[q] / total

    def last_alpha(q, alpha):
        potential = sq_x[q * CHUNK_T : (q + 1) * CHUNK_T, :] - EPS * jnp.log(total_f[q])
        for i in range(CHUNK_T // 2):
            f_ref[owner_rows(q * CHUNK_T // 2 + i), :] = potential[2 * i : 2 * i + 2]
        for t in range(CHUNK_T):
            at = q * CHUNK_T + t
            cols = slice(at * 128, (at + 1) * 128)
            x = xg[at // 2, :, (at % 2) * 128 : (at % 2 + 1) * 128].astype(F32) * alpha[t : t + 1, :]
            high = x.astype(BF16)
            coef[0:FEAT, cols] = high
            coef[FEAT : 2 * FEAT, cols] = (x - high.astype(F32)).astype(BF16)

    def fleet_pass(k):
        acc = tuple(jnp.zeros((8, 128), F32) for _ in range(FLEET_T))
        for q in range(CHUNKS):
            alpha = alpha_of(k, q)
            if k == ITERS - 1:
                last_alpha(q, alpha)
            with jax.named_scope("fleet_pass"):
                for t in range(CHUNK_T):
                    rows = slice(q * ROWS + t * 128, q * ROWS + (t + 1) * 128)
                    spread[rows, :] = jnp.broadcast_to(alpha[t : t + 1, :], (128, 128)).T

                def rows_of(r, acc):
                    rows = aligned(r * 8, 8, 8)
                    factor = spread[rows, :]
                    return tuple(acc[t] + e_ref[rows, t * 128 : (t + 1) * 128] * factor for t in range(FLEET_T))

                acc = lax.fori_loop(q * (ROWS // 8), (q + 1) * (ROWS // 8), rows_of, acc, unroll=8)
        for t in range(FLEET_T):
            g_send[k, fleet_row(t), :] = jnp.sum(acc[t], axis=0, keepdims=True)

    def start_fleet_sums(k):
        for n in reversed(range(LAB_N - 1)):
            copy_to_lab(n, g_send.at[k], g_recv.at[k, me_l], sent.at[3], g_rs.at[k]).start()
        g_recv[k, me_l] = g_send[k]

    def end_fleet_sums(k):
        with jax.named_scope("fleet_sums"):
            wait_received(g_recv.at[k, 0 : LAB_N - 1], g_rs.at[k])
        total = g_recv[k, 0]
        for p in range(1, LAB_N):
            total = total + g_recv[k, p]
        return total

    for k in range(ITERS - 1):
        fleet_pass(k)
        start_fleet_sums(k)
        total = end_fleet_sums(k)
        total = jnp.where((total > LOW) & (total < HIGH), total, jnp.nan)
        quotient[...] = b_ref[...] / total
        for t in range(FLEET_T):
            scale[t : t + 1, :] = quotient[fleet_row(t), :]
        lab_pass(k + 1)

    fleet_pass(ITERS - 1)
    mid = FLEET_T // 2
    for d in (2, 1, 3):
        copy_to_offset(0, d, g_send.at[ITERS - 1, 0:mid], gx.at[me_x], 8, t_rs.at[0]).start()
        copy_to_offset(d, 0, g_send.at[ITERS - 1, mid:FLEET_T], gz.at[me_z], 9, t_rs.at[1]).start()
    gx[me_x] = g_send[ITERS - 1, 0:mid]
    gz[me_z] = g_send[ITERS - 1, mid:FLEET_T]

    def forward_totals():
        with jax.named_scope("totals_first"):
            wait_received(gx.at[0:3], t_rs.at[0])
            wait_received(gz.at[0:3], t_rs.at[1])
        gx_sum[...] = sum_of([gx[i] for i in range(4)])
        gz_sum[...] = sum_of([gz[i] for i in range(4)])
        for d in (2, 1, 3):
            copy_to_offset(d, 0, gx_sum, gxz.at[me_z], 10, t_rs.at[2]).start()
            copy_to_offset(0, d, gz_sum, gzx.at[me_x], 11, t_rs.at[3]).start()
        gxz[me_z] = gx_sum[...]
        gzx[me_x] = gz_sum[...]


    def sum_of(parts):
        return (parts[0] + parts[1]) + (parts[2] + parts[3])

    def forward(offsets):
        with jax.named_scope("weighted_first"):
            for d in offsets:
                wait_received(wx.at[0:3, d], wx_rs.at[d])
                wx_sum[d - 1] = sum_of([wx[i, d] for i in range(4)])
                copy_to_offset(d, 0, wx_sum.at[d - 1], wxz.at[d - 1], 6, w_rs.at[0]).start()
                wait_received(wz.at[0:3, d], wz_rs.at[d])
                wz_sum[d - 1] = sum_of([wz[i, d] for i in range(4)])
                copy_to_offset(0, d, wz_sum.at[d - 1], wzx.at[d - 1], 7, w_rs.at[1]).start()

    for number, group in enumerate(GROUPS):
        with jax.named_scope("weighted"):
            for dz, dx in group:
                at = dz * 4 + dx
                slot = slot_from(dz, dx)
                cols = slice(slot * PIECE, (slot + 1) * PIECE)
                part = None
                for k in range(LAB // DEPTH):
                    rows = slice(k * DEPTH, (k + 1) * DEPTH)
                    e, left = e_ref[rows, cols], coef[:, rows]
                    high = e.astype(BF16)
                    term = dot(left, high) + dot(left, (e - high.astype(F32)).astype(BF16))
                    part = term if part is None else part + term
                weighted = part[:FEAT] + part[FEAT:]
                if dx == 0:
                    wx[3, dz] = weighted[:HALF]
                if dz == 0:
                    wz[3, dx] = weighted[HALF:]
                w_send[at] = weighted
            for dz, dx in group:
                at = dz * 4 + dx
                if dx != 0:
                    copy_to_offset(0, dx, w_send.at[at, 0:HALF], wx.at[dx - 1, dz], 4, wx_rs.at[dz]).start()
                if dz != 0:
                    copy_to_offset(dz, 0, w_send.at[at, HALF:FEAT], wz.at[dz - 1, dx], 5, wz_rs.at[dx]).start()

        if number == 2:
            forward_totals()
    forward((2, 1, 3))
    with jax.named_scope("totals_second"):
        wait_received(gxz.at[0:3], t_rs.at[2])
        wait_received(gzx.at[0:3], t_rs.at[3])
    scale[0:mid, :] = sum_of([gxz[i] for i in range(4)])
    scale[mid:FLEET_T, :] = sum_of([gzx[i] for i in range(4)])
    total = scale[...]
    flag_ref[0] = jnp.where(jnp.sum(jnp.where(total == total, 0.0, 1.0)) > 0.0, 1, 0)
    g_ref[...] = sq_y[...] - EPS * jnp.log(total)
    with jax.named_scope("weighted_own"):
        wait_received(wx.at[0:3, 0], wx_rs.at[0])
        wait_received(wz.at[0:3, 0], wz_rs.at[0])
    upper = sum_of([wx[i, 0] for i in range(4)])
    lower = sum_of([wz[i, 0] for i in range(4)])
    with jax.named_scope("weighted_second"):
        wait_received(wxz.at[0:3], w_rs.at[0])
        wait_received(wzx.at[0:3], w_rs.at[1])
    upper = sum_of([upper] + [wxz[i] for i in range(3)])
    lower = sum_of([lower] + [wzx[i] for i in range(3)])
    for h in range(2):
        cols = slice(h * 128, (h + 1) * 128)
        row = pl.ds(2 * me_l + h, 1)
        factor, inverse = 2.0 * b_ref[row, :], 1.0 / scale[row, :]
        for part, rows in ((upper, slice(0, HALF)), (lower, slice(HALF, FEAT))):
            grad_ref[rows, cols] = factor * (yg[LAB_OWN, rows, cols].astype(F32) - part[:, cols] * inverse)
    with jax.named_scope("outputs"):
        wait_sent(xg.at[0 : FLEET_N - 1], 0)
        wait_sent(yg.at[0 : LAB_N - 1], 1)
        wait_sent(f_recv.at[:, 0 : FLEET_N - 1], 2)
        wait_sent(g_recv.at[:, 0 : LAB_N - 1], 3)
        for i, slots in enumerate((wx, wz, wxz, wzx, gx, gz, gxz, gzx)):
            wait_sent(slots.at[0:3], 4 + i)


OUT_SHAPES = [
    jax.ShapeDtypeStruct((LAB_T, 128), F32),
    jax.ShapeDtypeStruct((FLEET_T, 128), F32),
    jax.ShapeDtypeStruct((FEAT, PIECE), F32),
]


def copy_kernel(*refs):
    for i in range(3):
        refs[3 + i][...] = refs[i][...]


def copy_outs(*outs):
    vmem = pl.BlockSpec(memory_space=pltpu.VMEM)
    return pl.pallas_call(
        copy_kernel, out_shape=OUT_SHAPES, in_specs=[vmem] * 3, out_specs=[vmem] * 3, name="outputs"
    )(*outs)


def scaled(lab_features, fleet_features, lab_weight, fleet_weight):
    anywhere = pl.BlockSpec(memory_space=pl.ANY)
    dma = pltpu.SemaphoreType.DMA
    return pl.pallas_call(
        kernel,
        out_shape=OUT_SHAPES + [jax.ShapeDtypeStruct((1,), jnp.int32)],
        in_specs=[anywhere] * 4,
        out_specs=[pl.BlockSpec(memory_space=pltpu.VMEM)] * 3 + [pl.BlockSpec(memory_space=pltpu.SMEM)],
        scratch_shapes=[
            pltpu.VMEM((LAB_T, 128), F32),
            pltpu.VMEM((FLEET_T, 128), F32),
            pltpu.VMEM((FLEET_N, FEAT, PIECE), BF16),
            pltpu.VMEM((LAB_N, FEAT, PIECE), BF16),
            pltpu.VMEM((LAB, FEAT), BF16),
            pltpu.VMEM((LAB, FLEET), F32),
            pltpu.VMEM((LAB, 128), F32),
            pltpu.VMEM((LAB, 128), F32),
            pltpu.VMEM((2 * FEAT, LAB), BF16),
            pltpu.VMEM((LAB_T, 128), F32),
            pltpu.VMEM((FLEET_T, 128), F32),
            pltpu.VMEM((FLEET_T, 128), F32),
            pltpu.VMEM((FLEET_T, 128), F32),
            pltpu.VMEM((CHUNKS, CHUNK_T, 128), F32),
            pltpu.VMEM((CHUNKS, CHUNK_T, 128), F32),
            pltpu.VMEM((ITERS, CHUNKS, CHUNK_T, 128), F32),
            pltpu.VMEM((ITERS, FLEET_N, CHUNKS, CHUNK_T, 128), F32),
            pltpu.VMEM((ITERS, FLEET_T, 128), F32),
            pltpu.VMEM((ITERS - 1, LAB_N, FLEET_T, 128), F32),
            pltpu.VMEM((4, FLEET_T // 2, 128), F32),
            pltpu.VMEM((4, FLEET_T // 2, 128), F32),
            pltpu.VMEM((FLEET_T // 2, 128), F32),
            pltpu.VMEM((FLEET_T // 2, 128), F32),
            pltpu.VMEM((4, FLEET_T // 2, 128), F32),
            pltpu.VMEM((4, FLEET_T // 2, 128), F32),
            pltpu.VMEM((LAB_N, FEAT, PIECE), F32),
            pltpu.VMEM((4, 4, HALF, PIECE), F32),
            pltpu.VMEM((4, 4, HALF, PIECE), F32),
            pltpu.VMEM((3, HALF, PIECE), F32),
            pltpu.VMEM((3, HALF, PIECE), F32),
            pltpu.VMEM((3, HALF, PIECE), F32),
            pltpu.VMEM((3, HALF, PIECE), F32),
            dma((4,)),
            dma((3,)),
            dma((ITERS, CHUNKS)),
            dma((ITERS - 1,)),
            dma((4,)),
            dma((4,)),
            dma((4,)),
            dma((2,)),
            dma((12,)),
            dma((4,)),
        ],
        name="sinkhorn",
        compiler_params=pltpu.CompilerParams(
            collective_id=0, has_side_effects=True, vmem_limit_bytes=56 * 2**20
        ),
    )(
        lab_features,
        fleet_features,
        lab_weight.reshape(LAB_T, 128),
        fleet_weight.reshape(FLEET_T, 128),
    )


def body(*args):
    *outs, flag = scaled(*args)

    def general():
        f, g, grad = log_domain(*args)
        return [f.reshape(LAB_T, 128), g.reshape(FLEET_T, 128), grad]

    f, g, grad = copy_outs(*lax.cond(flag[0] != 0, general, lambda: outs))
    return f.reshape(LAB), g.reshape(FLEET), grad


def solution(mesh):
    in_specs = (P(None, ("lab", "fleet")), P(None, ("fleet", "lab")), P("lab"), P("fleet"))
    out_specs = (P("lab"), P("fleet"), P(None, ("fleet", "lab")))
    return jax.shard_map(body, mesh=mesh, in_specs=in_specs, out_specs=out_specs, check_vma=False)
```

```python
import jax
import jax.numpy as jnp
from jax import lax
from jax.experimental import pallas as pl
from jax.experimental.pallas import tpu as pltpu
from jax.sharding import PartitionSpec as P


ITERS = 3
EPS = 0.5
LOG2E = 1.4426950408889634
LOW, HIGH = 2.0**-30, 2.0**60
LOW_RATIO, HIGH_RATIO = 2.0**-20, 2.0**20
MESH = pl.DeviceIdType.MESH
F32, BF16 = jnp.float32, jnp.bfloat16


def block_width():
    return 512


def split_columns(array, width):
    return array.reshape(array.shape[0], array.shape[1] // width, width).transpose(1, 0, 2)


def pair_cost(lab_part, sq_lab_part, fleet_part, sq_fleet_part):
    cross = lax.dot_general(
        lab_part, fleet_part, (((0,), (0,)), ((), ())), preferred_element_type=jnp.float32
    )
    return sq_lab_part[:, None] + sq_fleet_part[None, :] - 2.0 * cross


def square_sums(features):
    values = features.astype(jnp.float32)
    return jnp.sum(values * values, axis=0)


def ring(value, axis, visit, carry):
    n = lax.axis_size(axis)
    me = lax.axis_index(axis)

    right = [(i, (i + 1) % n) for i in range(n)]

    def step(k, state):
        block, carry = state
        carry = visit(lax.rem(me + n - k, n), block, carry)
        return lax.ppermute(block, axis, right), carry

    carry = visit(me, value, carry)
    return lax.fori_loop(1, n, step, (lax.ppermute(value, axis, right), carry))[1]


def gather(value, axis):
    def visit(index, block, out):
        return lax.dynamic_update_index_in_dim(out, block, index, 0)

    return ring(value, axis, visit, jnp.zeros((lax.axis_size(axis),) + value.shape, value.dtype))


def gather_columns(value, axis):
    return gather(value, axis).transpose(1, 0, 2).reshape(value.shape[0], -1)


def reduce_over(axis, top, total):
    tops, totals = gather(top, axis), gather(total, axis)
    top = jnp.max(tops, axis=0)
    total = jnp.sum(totals * jnp.exp(tops - top[None, :]), axis=0)
    return -EPS * (top + jnp.log(total))


def sum_own_columns(terms, axis):
    width = terms.shape[1] // lax.axis_size(axis)
    start = lax.axis_index(axis) * width

    def visit(index, block, out):
        return out + lax.dynamic_slice_in_dim(block, start, width, 1)

    return ring(terms, axis, visit, jnp.zeros((terms.shape[0], width), terms.dtype))


def log_domain(lab_features, fleet_features, lab_weight, fleet_weight):
    lab_block = gather_columns(lab_features, "fleet")
    fleet_block = gather_columns(fleet_features, "lab")
    sq_lab = square_sums(lab_block)
    sq_fleet = square_sums(fleet_block)
    log_a = jnp.log(lab_weight)
    log_b = jnp.log(fleet_weight)
    lab_count = lab_block.shape[1]
    fleet_count = fleet_block.shape[1]
    lab_width = block_width()
    fleet_width = block_width()
    lab_blocks = split_columns(lab_block, lab_width)
    fleet_blocks = split_columns(fleet_block, fleet_width)
    sq_lab_blocks = sq_lab.reshape(-1, lab_width)
    sq_fleet_blocks = sq_fleet.reshape(-1, fleet_width)
    log_b_blocks = log_b.reshape(-1, fleet_width)

    def lab_partial(fleet_pot):

        def lab_one_block(items):
            lab_part, sq_part = items
            score = (
                fleet_pot[None, :] - pair_cost(lab_part, sq_part, fleet_block, sq_fleet)
            ) / EPS + log_b[None, :]
            top = jnp.max(score, axis=1)
            return (top, jnp.sum(jnp.exp(score - top[:, None]), axis=1))

        top, total = lax.map(lab_one_block, (lab_blocks, sq_lab_blocks))
        return (top.reshape(lab_count), total.reshape(lab_count))

    def fleet_partial(lab_pot):

        def fleet_one_block(items):
            fleet_part, sq_part = items
            score = (
                lab_pot[:, None] - pair_cost(lab_block, sq_lab, fleet_part, sq_part)
            ) / EPS + log_a[:, None]
            top = jnp.max(score, axis=0)
            return (top, jnp.sum(jnp.exp(score - top[None, :]), axis=0))

        top, total = lax.map(fleet_one_block, (fleet_blocks, sq_fleet_blocks))
        return (top.reshape(fleet_count), total.reshape(fleet_count))

    def iteration(step, pots):
        lab_top, lab_total = lab_partial(pots[1])
        lab_pot = reduce_over("fleet", lab_top, lab_total)
        fleet_top, fleet_total = fleet_partial(lab_pot)
        return (lab_pot, reduce_over("lab", fleet_top, fleet_total))

    lab_pot, fleet_pot = lax.fori_loop(
        0, ITERS, iteration, (jnp.zeros((lab_count,), F32), jnp.zeros((fleet_count,), F32))
    )
    pot_blocks = fleet_pot.reshape(-1, fleet_width)
    lab_float = lab_block.astype(jnp.float32)

    def gradient_block(items):
        fleet_part, sq_part, pot_part, log_part = items
        cost = pair_cost(lab_block, sq_lab, fleet_part, sq_part)
        plan = jnp.exp(
            (lab_pot[:, None] + pot_part[None, :] - cost) / EPS + log_a[:, None] + log_part[None, :]
        )
        mass = jnp.sum(plan, axis=0)
        weighted = jnp.dot(
            lab_float, plan, preferred_element_type=jnp.float32, precision=lax.Precision.HIGHEST
        )
        return 2.0 * (fleet_part.astype(jnp.float32) * mass[None, :] - weighted)

    pieces = lax.map(gradient_block, (fleet_blocks, sq_fleet_blocks, pot_blocks, log_b_blocks))
    terms = pieces.transpose(1, 0, 2).reshape(fleet_block.shape[0], fleet_count)
    fleet_gradient = sum_own_columns(terms, "lab")
    return (lab_pot, fleet_pot, fleet_gradient)


FEAT = 64
PIECE = 256
LAB_N, FLEET_N = 16, 8
LAB, FLEET = PIECE * FLEET_N, PIECE * LAB_N
LAB_T, FLEET_T = LAB // 128, FLEET // 128
CHUNKS = 4
EXP_ROWS = 1024
HALF = FEAT // 2
ROWS = LAB // CHUNKS
CHUNK_T = LAB_T // CHUNKS
WAVE = FLEET_N // 2


def hops(offset):
    return sum(min(d, 4 - d) for d in offset)


LAB_OFFSETS = sorted(((z, x) for z in range(4) for x in range(4) if (z, x) != (0, 0)), key=hops)
LAB_OWN = LAB_N - 1
FLEET_OFFSETS = (4, 5, 3, 2, 6, 1, 7)
Y_OFFSETS = (2, 1, 3)
NEAR, MIDDLE, FAR = (LAB_OWN, 0, 1, 2, 3), (4, 5, 6, 7, 8, 9), (10, 11, 12, 13, 14)
GROUPS = (
    ((2, 2),),
    ((2, 1), (1, 2)),
    ((2, 3), (3, 2)),
    ((1, 1), (1, 3), (3, 1), (3, 3)),
    ((0, 2), (2, 0), (0, 1), (1, 0)),
    ((0, 3), (3, 0), (0, 0)),
)
DEPTH = 256


def slot_from(dz, dx):
    back = (-dz % 4, -dx % 4)
    return LAB_OWN if back == (0, 0) else LAB_OFFSETS.index(back)


def owner_rows(position):
    piece = (position % WAVE) * 2 + position // WAVE
    return slice(2 * piece, 2 * piece + 2)


def dot(left, right):
    return lax.dot_general(left, right, (((1,), (0,)), ((), ())), preferred_element_type=F32)


def aligned(start, size, multiple):
    return pl.ds(pl.multiple_of(start, multiple), size)


def kernel(
    x_in, y_in, a_in, b_in, f_ref, g_ref, grad_ref, flag_ref,
    a_ref, b_ref,
    xg, yg, xt, e_ref, lanes, spread, coef, sq_x, sq_y, scale, quotient, a_own, total_f, f_send, f_recv, g_send, g_recv,
    gx, gz, gx_sum, gz_sum, gxz, gzx, w_send, wx, wz, wx_sum, wz_sum, wxz, wzx,
    x_rs, y_rs, f_rs, g_rs, t_rs, wx_rs, wz_rs, w_rs, sent, in_s,
):
    me_l, me_f = lax.axis_index("lab"), lax.axis_index("fleet")
    core, chip = lax.rem(me_f, 2), me_f // 2
    me_z, me_x = me_l // 4, lax.rem(me_l, 4)

    def lab_at(dz, dx):
        return lax.rem(me_z + dz, 4) * 4 + lax.rem(me_x + dx, 4)

    fleet_to = [lax.rem(me_f + d, FLEET_N) for d in FLEET_OFFSETS]
    lab_to = [lab_at(dz, dx) for dz, dx in LAB_OFFSETS] + [me_l]
    lab_from = [lab_at(4 - dz, 4 - dx) for dz, dx in LAB_OFFSETS] + [me_l]

    barrier = pltpu.get_barrier_semaphore()
    for p in reversed(lab_to[:LAB_OWN]):
        pl.semaphore_signal(barrier, inc=1, device_id=(p, me_f), device_id_type=MESH)
    for p in fleet_to:
        pl.semaphore_signal(barrier, inc=1, device_id=(me_l, p), device_id_type=MESH)
    mine = core * WAVE + chip
    pairs = ((x_in, xg.at[mine]), (y_in, yg.at[LAB_OWN]), (a_in, a_ref), (b_in, b_ref))
    loads = [pltpu.make_async_copy(src, dst, in_s.at[i]) for i, (src, dst) in enumerate(pairs)]
    for c in loads:
        c.start()
    for c in loads:
        c.wait()
    with jax.named_scope("barrier"):
        pl.semaphore_wait(barrier, LAB_N - 1 + FLEET_N - 1)

    def copy_to_lab(n, src, dst, send, recv):
        return pltpu.make_async_remote_copy(
            src_ref=src, dst_ref=dst, send_sem=send, recv_sem=recv,
            device_id=(lab_to[n], me_f), device_id_type=MESH,
        )

    def copy_to_offset(dz, dx, src, dst, send, recv):
        return pltpu.make_async_remote_copy(
            src_ref=src, dst_ref=dst, send_sem=sent.at[send], recv_sem=recv,
            device_id=(lab_at(dz, dx), me_f), device_id_type=MESH,
        )

    def copy_to_fleet(to, src, dst, send, recv):
        return pltpu.make_async_remote_copy(
            src_ref=src, dst_ref=dst, send_sem=send, recv_sem=recv,
            device_id=(me_l, to), device_id_type=MESH,
        )

    def wait_sent(slots, send):
        copy_to_lab(0, slots, slots, sent.at[send], sent.at[send]).wait_send()

    def wait_received(slots, recv):
        copy_to_lab(0, slots, slots, sent.at[0], recv).wait_recv()

    sibling = chip * 2 + 1 - core
    x_copies = [
        copy_to_fleet(lax.rem(chip + d, 4) * 2 + core, xg.at[mine], xg.at[mine], sent.at[0], x_rs.at[n])
        for n, d in enumerate(Y_OFFSETS)
    ]
    x_copies.append(copy_to_fleet(sibling, xg.at[mine], xg.at[mine], sent.at[0], x_rs.at[3]))
    y_copies = [
        copy_to_lab(n, yg.at[LAB_OWN], yg.at[n], sent.at[1], y_rs.at[0 if n in NEAR else 1 if n in MIDDLE else 2]) for n in range(LAB_N - 1)
    ]
    for c in x_copies + y_copies:
        c.start()
    for at in range(FLEET_N):
        q, i = divmod(2 * at, CHUNK_T)
        a_own[q, i : i + 2, :] = a_ref[owner_rows(at), :]

    def fleet_row(t):
        return pl.ds(2 * lab_from[t // 2] + t % 2, 1)

    def x_prep(at):
        x = xg[at].astype(F32)
        xt[aligned(at * PIECE, PIECE, PIECE), :] = x.T.astype(BF16)
        sq = jnp.sum(x * x, axis=0, keepdims=True)
        for h in range(2):
            sq_x[pl.ds(2 * at + h, 1), :] = sq[:, h * 128 : (h + 1) * 128]

    def y_prep(n):
        y = yg[n].astype(F32)
        sq = jnp.sum(y * y, axis=0, keepdims=True)
        for h in range(2):
            row = fleet_row(2 * n + h)
            part = sq[:, h * 128 : (h + 1) * 128]
            sq_y[row, :] = part
            scale[2 * n + h : 2 * n + h + 1, :] = b_ref[row, :] * jnp.exp2(part * (-LOG2E / EPS))

    def exp_rows(start, size, slots, first):
        rows = aligned(start, size, size)
        left = xt[rows, :]
        total = None if first else lanes[rows, :]
        for n in slots:
            part = jnp.exp2(dot(left, yg[n]) * (2.0 * LOG2E / EPS))
            e_ref[rows, n * PIECE : (n + 1) * PIECE] = part
            for h in range(2):
                term = part[:, h * 128 : (h + 1) * 128] * scale[2 * n + h : 2 * n + h + 1, :]
                total = term if total is None else total + term
        lanes[rows, :] = total

    def copy_sums(k, q, n):
        return copy_to_fleet(fleet_to[n], f_send.at[k, q], f_recv.at[k, me_f, q], sent.at[2], f_rs.at[k, q])

    def send_sums(k, q):
        for t in range(CHUNK_T):
            rows = aligned(q * ROWS + t * 128, 128, 128)
            f_send[k, q, t : t + 1, :] = jnp.sum(lanes[rows, :].T, axis=0, keepdims=True)
        for n in range(FLEET_N - 1):
            copy_sums(k, q, n).start()
        f_recv[k, me_f, q] = f_send[k, q]

    y_prep(LAB_OWN)
    x_prep(mine)
    with jax.named_scope("x_wait"):
        for n in (1, 2, 0):
            d = Y_OFFSETS[n]
            x_copies[n].wait_recv()
            at = core * WAVE + lax.rem(chip + 4 - d, 4)
            copy_to_fleet(sibling, xg.at[at], xg.at[at], sent.at[0], x_rs.at[3]).start()
        for d in Y_OFFSETS:
            x_prep(core * WAVE + lax.rem(chip + 4 - d, 4))
    with jax.named_scope("y_near"):
        wait_received(yg.at[0 : len(NEAR) - 1], y_rs.at[0])
        for n in NEAR[1:]:
            y_prep(n)
    with jax.named_scope("exp_first"):
        exp_rows(core * EXP_ROWS, EXP_ROWS, NEAR, True)
    with jax.named_scope("y_middle"):
        wait_received(yg.at[0 : len(MIDDLE)], y_rs.at[1])
        for n in MIDDLE:
            y_prep(n)
    with jax.named_scope("exp_middle"):
        exp_rows(core * EXP_ROWS, EXP_ROWS, MIDDLE, False)
    with jax.named_scope("x_sibling"):
        wait_received(xg.at[0:WAVE], x_rs.at[3])
        for i in range(WAVE):
            x_prep((1 - core) * WAVE + i)
    with jax.named_scope("exp_second"):
        exp_rows((1 - core) * EXP_ROWS, EXP_ROWS, NEAR + MIDDLE, True)
    with jax.named_scope("y_far"):
        wait_received(yg.at[0 : len(FAR)], y_rs.at[2])
        for n in FAR:
            y_prep(n)

    def exp_far(q, carry):
        exp_rows(q * ROWS, ROWS, FAR, False)
        send_sums(0, q)
        return carry

    with jax.named_scope("exp_far"):
        lax.fori_loop(0, CHUNKS, exp_far, 0)

    def lab_pass(k):
        beta = [jnp.broadcast_to(scale[t : t + 1, :], (8, 128)) for t in range(FLEET_T)]

        def rows_of(r, carry):
            for i in range(8):
                rows = aligned(r * 64 + 8 * i, 8, 8)
                acc = [e_ref[rows, t * 128 : (t + 1) * 128] * beta[t] for t in range(4)]
                for t in range(4, FLEET_T):
                    acc[t % 4] = acc[t % 4] + e_ref[rows, t * 128 : (t + 1) * 128] * beta[t]
                lanes[rows, :] = (acc[0] + acc[1]) + (acc[2] + acc[3])
            return carry

        def chunk(q, carry):
            lax.fori_loop(q * (ROWS // 64), (q + 1) * (ROWS // 64), rows_of, 0)
            send_sums(k, q)
            return carry

        with jax.named_scope("lab_pass"):
            lax.fori_loop(0, CHUNKS, chunk, 0)

    def alpha_of(k, q):
        with jax.named_scope("lab_sums"):
            wait_received(f_recv.at[k, 0 : FLEET_N - 1, q], f_rs.at[k, q])
        total = f_recv[k, 0, q]
        for p in range(1, FLEET_N):
            total = total + f_recv[k, p, q]
        good = (total > LOW) & (total < HIGH)
        if k > 0:
            before = total_f[q]
            good = good & (total > before * LOW_RATIO) & (total < before * HIGH_RATIO)
        total = jnp.where(good, total, jnp.nan)
        total_f[q] = total
        return a_own[q] / total

    def last_alpha(q, alpha):
        potential = sq_x[q * CHUNK_T : (q + 1) * CHUNK_T, :] - EPS * jnp.log(total_f[q])
        for i in range(CHUNK_T // 2):
            f_ref[owner_rows(q * CHUNK_T // 2 + i), :] = potential[2 * i : 2 * i + 2]
        for t in range(CHUNK_T):
            at = q * CHUNK_T + t
            cols = slice(at * 128, (at + 1) * 128)
            x = xg[at // 2, :, (at % 2) * 128 : (at % 2 + 1) * 128].astype(F32) * alpha[t : t + 1, :]
            high = x.astype(BF16)
            coef[0:FEAT, cols] = high
            coef[FEAT : 2 * FEAT, cols] = (x - high.astype(F32)).astype(BF16)

    def fleet_pass(k):
        acc = tuple(jnp.zeros((8, 128), F32) for _ in range(FLEET_T))
        for q in range(CHUNKS):
            alpha = alpha_of(k, q)
            if k == ITERS - 1:
                last_alpha(q, alpha)
            with jax.named_scope("fleet_pass"):
                for t in range(CHUNK_T):
                    rows = slice(q * ROWS + t * 128, q * ROWS + (t + 1) * 128)
                    spread[rows, :] = jnp.broadcast_to(alpha[t : t + 1, :], (128, 128)).T

                def rows_of(r, acc):
                    rows = aligned(r * 8, 8, 8)
                    factor = spread[rows, :]
                    return tuple(acc[t] + e_ref[rows, t * 128 : (t + 1) * 128] * factor for t in range(FLEET_T))

                acc = lax.fori_loop(q * (ROWS // 8), (q + 1) * (ROWS // 8), rows_of, acc, unroll=8)
        for t in range(FLEET_T):
            g_send[k, fleet_row(t), :] = jnp.sum(acc[t], axis=0, keepdims=True)

    def start_fleet_sums(k):
        for n in reversed(range(LAB_N - 1)):
            copy_to_lab(n, g_send.at[k], g_recv.at[k, me_l], sent.at[3], g_rs.at[k]).start()
        g_recv[k, me_l] = g_send[k]

    def end_fleet_sums(k):
        with jax.named_scope("fleet_sums"):
            wait_received(g_recv.at[k, 0 : LAB_N - 1], g_rs.at[k])
        total = g_recv[k, 0]
        for p in range(1, LAB_N):
            total = total + g_recv[k, p]
        return total

    for k in range(ITERS - 1):
        fleet_pass(k)
        start_fleet_sums(k)
        total = end_fleet_sums(k)
        total = jnp.where((total > LOW) & (total < HIGH), total, jnp.nan)
        quotient[...] = b_ref[...] / total
        for t in range(FLEET_T):
            scale[t : t + 1, :] = quotient[fleet_row(t), :]
        lab_pass(k + 1)

    fleet_pass(ITERS - 1)
    mid = FLEET_T // 2
    for d in (2, 1, 3):
        copy_to_offset(0, d, g_send.at[ITERS - 1, 0:mid], gx.at[me_x], 8, t_rs.at[0]).start()
        copy_to_offset(d, 0, g_send.at[ITERS - 1, mid:FLEET_T], gz.at[me_z], 9, t_rs.at[1]).start()
    gx[me_x] = g_send[ITERS - 1, 0:mid]
    gz[me_z] = g_send[ITERS - 1, mid:FLEET_T]

    def forward_totals():
        with jax.named_scope("totals_first"):
            wait_received(gx.at[0:3], t_rs.at[0])
            wait_received(gz.at[0:3], t_rs.at[1])
        gx_sum[...] = sum_of([gx[i] for i in range(4)])
        gz_sum[...] = sum_of([gz[i] for i in range(4)])
        for d in (2, 1, 3):
            copy_to_offset(d, 0, gx_sum, gxz.at[me_z], 10, t_rs.at[2]).start()
            copy_to_offset(0, d, gz_sum, gzx.at[me_x], 11, t_rs.at[3]).start()
        gxz[me_z] = gx_sum[...]
        gzx[me_x] = gz_sum[...]


    def sum_of(parts):
        return (parts[0] + parts[1]) + (parts[2] + parts[3])

    def forward(offsets):
        with jax.named_scope("weighted_first"):
            for d in offsets:
                wait_received(wx.at[0:3, d], wx_rs.at[d])
                wx_sum[d - 1] = sum_of([wx[i, d] for i in range(4)])
                copy_to_offset(d, 0, wx_sum.at[d - 1], wxz.at[d - 1], 6, w_rs.at[0]).start()
                wait_received(wz.at[0:3, d], wz_rs.at[d])
                wz_sum[d - 1] = sum_of([wz[i, d] for i in range(4)])
                copy_to_offset(0, d, wz_sum.at[d - 1], wzx.at[d - 1], 7, w_rs.at[1]).start()

    for number, group in enumerate(GROUPS):
        with jax.named_scope("weighted"):
            for dz, dx in group:
                at = dz * 4 + dx
                slot = slot_from(dz, dx)
                cols = slice(slot * PIECE, (slot + 1) * PIECE)
                part = None
                for k in range(LAB // DEPTH):
                    rows = slice(k * DEPTH, (k + 1) * DEPTH)
                    e, left = e_ref[rows, cols], coef[:, rows]
                    high = e.astype(BF16)
                    term = dot(left, high) + dot(left, (e - high.astype(F32)).astype(BF16))
                    part = term if part is None else part + term
                weighted = part[:FEAT] + part[FEAT:]
                if dx == 0:
                    wx[3, dz] = weighted[:HALF]
                if dz == 0:
                    wz[3, dx] = weighted[HALF:]
                w_send[at] = weighted
            for dz, dx in group:
                at = dz * 4 + dx
                if dx != 0:
                    copy_to_offset(0, dx, w_send.at[at, 0:HALF], wx.at[dx - 1, dz], 4, wx_rs.at[dz]).start()
                if dz != 0:
                    copy_to_offset(dz, 0, w_send.at[at, HALF:FEAT], wz.at[dz - 1, dx], 5, wz_rs.at[dx]).start()

        if number == 3:
            forward_totals()
    forward((2, 1, 3))
    with jax.named_scope("totals_second"):
        wait_received(gxz.at[0:3], t_rs.at[2])
        wait_received(gzx.at[0:3], t_rs.at[3])
    scale[0:mid, :] = sum_of([gxz[i] for i in range(4)])
    scale[mid:FLEET_T, :] = sum_of([gzx[i] for i in range(4)])
    total = scale[...]
    flag_ref[0] = jnp.where(jnp.sum(jnp.where(total == total, 0.0, 1.0)) > 0.0, 1, 0)
    g_ref[...] = sq_y[...] - EPS * jnp.log(total)
    with jax.named_scope("weighted_own"):
        wait_received(wx.at[0:3, 0], wx_rs.at[0])
        wait_received(wz.at[0:3, 0], wz_rs.at[0])
    upper = sum_of([wx[i, 0] for i in range(4)])
    lower = sum_of([wz[i, 0] for i in range(4)])
    with jax.named_scope("sent"):
        wait_sent(xg.at[0 : FLEET_N - 1], 0)
        wait_sent(yg.at[0 : LAB_N - 1], 1)
        wait_sent(f_recv.at[:, 0 : FLEET_N - 1], 2)
        wait_sent(g_recv.at[:, 0 : LAB_N - 1], 3)
        for i, slots in enumerate((wx, wz, wxz, wzx, gx, gz, gxz, gzx)):
            wait_sent(slots.at[0:3], 4 + i)
    with jax.named_scope("weighted_second"):
        wait_received(wxz.at[0:3], w_rs.at[0])
        wait_received(wzx.at[0:3], w_rs.at[1])
    upper = sum_of([upper] + [wxz[i] for i in range(3)])
    lower = sum_of([lower] + [wzx[i] for i in range(3)])
    for h in range(2):
        cols = slice(h * 128, (h + 1) * 128)
        row = pl.ds(2 * me_l + h, 1)
        factor, inverse = 2.0 * b_ref[row, :], 1.0 / scale[row, :]
        for part, rows in ((upper, slice(0, HALF)), (lower, slice(HALF, FEAT))):
            grad_ref[rows, cols] = factor * (yg[LAB_OWN, rows, cols].astype(F32) - part[:, cols] * inverse)


OUT_SHAPES = [
    jax.ShapeDtypeStruct((LAB_T, 128), F32),
    jax.ShapeDtypeStruct((FLEET_T, 128), F32),
    jax.ShapeDtypeStruct((FEAT, PIECE), F32),
]


def copy_kernel(*refs):
    for i in range(3):
        refs[3 + i][...] = refs[i][...]


def copy_outs(*outs):
    vmem = pl.BlockSpec(memory_space=pltpu.VMEM)
    return pl.pallas_call(
        copy_kernel, out_shape=OUT_SHAPES, in_specs=[vmem] * 3, out_specs=[vmem] * 3, name="outputs"
    )(*outs)


def scaled(lab_features, fleet_features, lab_weight, fleet_weight):
    anywhere = pl.BlockSpec(memory_space=pl.ANY)
    dma = pltpu.SemaphoreType.DMA
    return pl.pallas_call(
        kernel,
        out_shape=OUT_SHAPES + [jax.ShapeDtypeStruct((1,), jnp.int32)],
        in_specs=[anywhere] * 4,
        out_specs=[pl.BlockSpec(memory_space=pltpu.VMEM)] * 3 + [pl.BlockSpec(memory_space=pltpu.SMEM)],
        scratch_shapes=[
            pltpu.VMEM((LAB_T, 128), F32),
            pltpu.VMEM((FLEET_T, 128), F32),
            pltpu.VMEM((FLEET_N, FEAT, PIECE), BF16),
            pltpu.VMEM((LAB_N, FEAT, PIECE), BF16),
            pltpu.VMEM((LAB, FEAT), BF16),
            pltpu.VMEM((LAB, FLEET), F32),
            pltpu.VMEM((LAB, 128), F32),
            pltpu.VMEM((LAB, 128), F32),
            pltpu.VMEM((2 * FEAT, LAB), BF16),
            pltpu.VMEM((LAB_T, 128), F32),
            pltpu.VMEM((FLEET_T, 128), F32),
            pltpu.VMEM((FLEET_T, 128), F32),
            pltpu.VMEM((FLEET_T, 128), F32),
            pltpu.VMEM((CHUNKS, CHUNK_T, 128), F32),
            pltpu.VMEM((CHUNKS, CHUNK_T, 128), F32),
            pltpu.VMEM((ITERS, CHUNKS, CHUNK_T, 128), F32),
            pltpu.VMEM((ITERS, FLEET_N, CHUNKS, CHUNK_T, 128), F32),
            pltpu.VMEM((ITERS, FLEET_T, 128), F32),
            pltpu.VMEM((ITERS - 1, LAB_N, FLEET_T, 128), F32),
            pltpu.VMEM((4, FLEET_T // 2, 128), F32),
            pltpu.VMEM((4, FLEET_T // 2, 128), F32),
            pltpu.VMEM((FLEET_T // 2, 128), F32),
            pltpu.VMEM((FLEET_T // 2, 128), F32),
            pltpu.VMEM((4, FLEET_T // 2, 128), F32),
            pltpu.VMEM((4, FLEET_T // 2, 128), F32),
            pltpu.VMEM((LAB_N, FEAT, PIECE), F32),
            pltpu.VMEM((4, 4, HALF, PIECE), F32),
            pltpu.VMEM((4, 4, HALF, PIECE), F32),
            pltpu.VMEM((3, HALF, PIECE), F32),
            pltpu.VMEM((3, HALF, PIECE), F32),
            pltpu.VMEM((3, HALF, PIECE), F32),
            pltpu.VMEM((3, HALF, PIECE), F32),
            dma((4,)),
            dma((3,)),
            dma((ITERS, CHUNKS)),
            dma((ITERS - 1,)),
            dma((4,)),
            dma((4,)),
            dma((4,)),
            dma((2,)),
            dma((12,)),
            dma((4,)),
        ],
        name="sinkhorn",
        compiler_params=pltpu.CompilerParams(
            collective_id=0, has_side_effects=True, vmem_limit_bytes=42 * 2**20
        ),
    )(
        lab_features,
        fleet_features,
        lab_weight.reshape(LAB_T, 128),
        fleet_weight.reshape(FLEET_T, 128),
    )


def body(*args):
    *outs, flag = scaled(*args)

    def general():
        f, g, grad = log_domain(*args)
        return [f.reshape(LAB_T, 128), g.reshape(FLEET_T, 128), grad]

    f, g, grad = copy_outs(*lax.cond(flag[0] != 0, general, lambda: outs))
    return f.reshape(LAB), g.reshape(FLEET), grad


def solution(mesh):
    in_specs = (P(None, ("lab", "fleet")), P(None, ("fleet", "lab")), P("lab"), P("fleet"))
    out_specs = (P("lab"), P("fleet"), P(None, ("fleet", "lab")))
    return jax.shard_map(body, mesh=mesh, in_specs=in_specs, out_specs=out_specs, check_vma=False)
```
